512 devices in a mesh: pair: 32 (over y, z_lo), virt: 16 (over x, z_hi, core).
Axes of the slice: x: 4, y: 8, z: 8 (z_hi: 2, z_lo: 4; z = z_hi * 4 + z_lo), core: 2. Of those that a mesh axis runs over, the one named last changes fastest.
Arguments:
- amplitudes: bfloat16 [16384, 6144], P('pair', 'virt'), may hold values from -6 to 6
- integrals: bfloat16 [6144, 6144], P('pair', 'virt'), may hold values from -0.21875 to 0.21875
- irreps: int32 [768], replicated, may hold values from 0 to 7, as said below
Outputs:
- ladder: bfloat16 [16384, 6144], P('pair', 'virt')
The draws below stay inside these ranges and needn't reach their ends.
Inputs may be any that keep to these rules, and one draw needn't show every extreme that they name: irreps never falls along the orbitals; each irrep 0 to 7 occupies one block of one or more whole tiles of 64 orbitals, and every irrep appears.
All inputs are finite; a program needn't handle non-finite values.
Results may differ from the reference program's by a relative error of at most 0.001.
Values may be sent and summed in bfloat16 or wider, within the bound.
A program may use at most 64 MiB of HBM per device.

```python
import jax
import jax.numpy as jnp

NVIR = 768
PAIRS = 16384
KROWS = 6144
NCOLS = 6144


def draw_irreps(key, part):
    key = jax.random.fold_in(key, 3)
    tile_count = 12
    extra_tiles = jax.random.randint(key, (4,), 0, 8)
    labels = jnp.arange(8, dtype=jnp.int32)
    counts = 1 + jnp.sum((extra_tiles[:, None] == labels[None, :]).astype(jnp.int32), axis=0)
    block_ends = jnp.cumsum(counts).astype(jnp.int32)
    tile_ids = jnp.arange(tile_count, dtype=jnp.int32)
    tile_irrep = jnp.sum((tile_ids[:, None] >= block_ends[None, :]).astype(jnp.int32), axis=1)
    tile_width = NVIR // tile_count
    orbital = jnp.arange(NVIR, dtype=jnp.int32)
    return tile_irrep[orbital // tile_width].astype(jnp.int32)


def level_of(stream_key, shape, cuts, low, high):
    factor_of, own = 1.0, jax.random.fold_in(stream_key, 6)
    for dim, parts in cuts:
        draws = jnp.exp(jax.random.uniform(jax.random.fold_in(own, dim), (parts,), jnp.float32, low / len(cuts), high / len(cuts)))
        factor_of = factor_of * jnp.repeat(draws, shape[dim] // parts).reshape([-1 if axis == dim else 1 for axis in range(len(shape))])
    return factor_of


def normal_values(rng, extent, width, bound, split=(), kind=jnp.bfloat16):
    factor_of = level_of(rng, extent, split, -0.22, 0.18) if split else 1.0
    values = jax.random.normal(rng, extent, jnp.float32) * width * factor_of
    return jnp.minimum(jnp.maximum(values, -bound), bound).astype(kind)


def setup_inputs(seed: int = 0) -> dict:
    splits = jax.random.split(jax.random.key(seed), 4)
    amplitudes = normal_values(splits[0], (PAIRS, KROWS), 1.0, 6.0, ((0, 32), (1, 16)))
    integrals = normal_values(splits[1], (KROWS, NCOLS), (KROWS // 8) ** -0.5, 0.21875, ((0, 32), (1, 16)))
    irreps = draw_irreps(jax.random.fold_in(splits[3], 71), 0)
    return dict(amplitudes=amplitudes, integrals=integrals, irreps=irreps)


def reference(amplitudes, integrals, irreps):
    nvir = irreps.shape[0]
    slab_c = amplitudes.shape[1] // nvir
    slab_a = integrals.shape[1] // nvir
    row_sym = jnp.bitwise_xor(irreps[:slab_c, None], irreps[None, :]).reshape(-1)
    col_sym = jnp.bitwise_xor(irreps[:slab_a, None], irreps[None, :]).reshape(-1)
    allowed = jnp.where(row_sym[:, None] == col_sym[None, :], integrals, jnp.zeros_like(integrals))
    ladder = jnp.dot(amplitudes, allowed, preferred_element_type=jnp.float32)
    return ladder.astype(jnp.bfloat16)
```

```python
import jax
import jax.numpy as jnp
from jax import lax
from jax.experimental import pallas as pl
from jax.experimental.pallas import tpu as pltpu
from jax.sharding import PartitionSpec as P

MESH = pl.DeviceIdType.MESH
BF16 = jnp.bfloat16
F32 = jnp.float32
TILE = 64
TILES = 12
BINS = 4
BIN = 192
NVIR = 768
HALF = 384
CHUNKS = 4
RC = 64
ROWS = 256


def slot_of_tiles(irreps_ref):
    irrep = [irreps_ref[TILE * i] for i in range(TILES)]
    count = [sum((irrep[i] == g).astype(jnp.int32) for i in range(TILES)) for g in range(8)]
    three = [(c == 3).astype(jnp.int32) for c in count]
    two = [(c == 2).astype(jnp.int32) for c in count]
    one = [(c == 1).astype(jnp.int32) for c in count]
    n3, n2 = sum(three), sum(two)
    slots = [jnp.int32(0)] * TILES
    start = r3 = r2 = r1 = jnp.int32(0)
    for g in range(8):
        lone = jnp.where(r1 < n2, 3 * (n3 + r1) + 2, 3 * (n3 + n2) + r1 - n2)
        base = jnp.where(three[g] == 1, 3 * r3, jnp.where(two[g] == 1, 3 * (n3 + r2), lone))
        for i in range(TILES):
            slots[i] = jnp.where(irrep[i] == g, base + i - start, slots[i])
        start, r3, r2, r1 = start + count[g], r3 + three[g], r2 + two[g], r1 + one[g]
    return irrep, slots


def kernel(
    t_ref, v_ref, irreps_ref, out_ref,
    traw, tpart, tsend, trecv, vraw, vpack, vsend, vrecv, vall, osend, orecv, ofull,
    pick, vpick, vrow, unpick,
    send_sem, recv_sem, local_sem,
):
    pair, virt = lax.axis_index("pair"), lax.axis_index("virt")
    y, zl = pair // 4, pair % 4
    x, zh, k = virt // 4, (virt // 2) % 2, virt % 2

    def device(x=x, y=y, zh=zh, zl=zl, k=k):
        return (y * 4 + zl, (x * 2 + zh) * 2 + k)

    xs = [(x + j) % 4 for j in (1, 3, 2)]
    zs = [(zl + j) % 4 for j in (1, 2, 3)]
    up, down = (y + 1) % 8, (y + 7) % 8
    peers = (
        [device(k=1 - k), device(zh=1 - zh), device(zh=1 - zh, k=1 - k)]
        + [device(x=o) for o in xs] + [device(zl=o) for o in zs] + [device(y=up), device(y=down)]
    )
    barrier = pltpu.get_barrier_semaphore()
    for peer in peers:
        pl.semaphore_signal(barrier, inc=1, device_id=peer, device_id_type=MESH)
    pl.semaphore_wait(barrier, len(peers))

    used = [0]
    sent = []

    def send(src, dst, to):
        n = used[0]
        used[0] += 1
        copy = pltpu.make_async_remote_copy(
            src_ref=src, dst_ref=dst, send_sem=send_sem.at[n], recv_sem=recv_sem.at[n],
            device_id=to, device_id_type=MESH,
        )
        copy.start()
        sent.append(copy)
        return copy

    mine = pl.multiple_of(k * HALF, HALF)
    theirs = pl.multiple_of((1 - k) * HALF, HALF)
    vmine, vtheirs = pl.multiple_of(k * 96, 32), pl.multiple_of((1 - k) * 96, 32)
    tmine, ttheirs = pl.multiple_of(k * ROWS, ROWS), pl.multiple_of((1 - k) * ROWS, ROWS)
    other = device(k=1 - k)

    vraw_copy = send(v_ref.at[pl.ds(vtheirs, 96), :], vraw.at[:, pl.ds(mine, HALF)], other)
    own_copies, far_copies = [], []
    for j in range(CHUNKS):
        rows = pl.ds(ttheirs + j * RC, RC)
        own_copies.append(send(t_ref.at[rows, :], traw.at[0, j, :, pl.ds(mine, HALF)], other))
    for j in range(CHUNKS):
        pair_copies = []
        pair_copies.append(
            send(t_ref.at[pl.ds(tmine + j * RC, RC), :], traw.at[1, j, :, pl.ds(mine, HALF)], device(zh=1 - zh))
        )
        pair_copies.append(
            send(t_ref.at[pl.ds(ttheirs + j * RC, RC), :], traw.at[1, j, :, pl.ds(mine, HALF)],
                 device(zh=1 - zh, k=1 - k))
        )
        far_copies.append(pair_copies)
    vraw[:, pl.ds(mine, HALF)] = v_ref[pl.ds(vmine, 96), :]
    for j in range(CHUNKS):
        traw[0, j, :, pl.ds(mine, HALF)] = t_ref[pl.ds(tmine + j * RC, RC), :]

    irrep, slots = slot_of_tiles(irreps_ref)
    bins = [s // 3 for s in slots]
    places = [(s % 3) * TILE for s in slots]

    shift = (x % 2) * TILE
    diff = lax.broadcasted_iota(jnp.int32, (TILE, 1024), 1) - lax.broadcasted_iota(jnp.int32, (TILE, 1024), 0)
    for i in range(TILES):
        vpick[pl.ds(i * TILE, TILE), :] = jnp.where(diff == bins[i] * 256 + shift + places[i], 1.0, 0.0).astype(BF16)
    lane = lax.broadcasted_iota(jnp.int32, (1, 1024), 1)
    lane_irrep = jnp.full((1, 1024), -1, jnp.int32)
    for i in range(TILES):
        at = bins[i] * 256 + shift + places[i]
        lane_irrep = jnp.where((lane >= at) & (lane < at + TILE), irrep[i], lane_irrep)

    vraw_copy.wait_recv()
    packed = jnp.dot(vraw[...], vpick[...], preferred_element_type=F32)
    for j in range(3):
        row_irrep = irreps_ref[TILE * (3 * zl + (k * 3 + j) // 2)]
        part = jnp.where(lane_irrep == row_irrep, packed[j * 32:(j + 1) * 32, :], 0.0)
        part = part[:, 0:256] + part[:, 256:512] + part[:, 512:768] + part[:, 768:1024]
        vpack[zl, k, pl.ds(j * 32, 32), :] = part.astype(BF16)
    mypack = vpack.at[zl, k]
    zcopies = [send(mypack, mypack, device(zl=o)) for o in zs]
    dcopies = [send(mypack, mypack, other)]

    olane = lax.broadcasted_iota(jnp.int32, (1, NVIR), 1)
    oslot = jnp.zeros((1, NVIR), jnp.int32)
    opad = jnp.zeros((1, NVIR), jnp.int32)
    for i in range(TILES):
        here = (olane >= i * TILE) & (olane < (i + 1) * TILE)
        oslot = jnp.where(here, slots[i] * TILE + olane - i * TILE, oslot)
        opad = jnp.where(here, bins[i] * 256 + places[i] + olane - i * TILE, opad)
    for m in range(BINS):
        want = lax.broadcasted_iota(jnp.int32, (96, NVIR), 0) + m * BIN + k * 96
        vrow[pl.ds(m * 96, 96), :] = jnp.where(want == oslot, 1.0, 0.0).astype(BF16)

    for j, o in enumerate(zs):
        source = (zl + 4 - (1, 2, 3)[j]) % 4
        zcopies[j].wait_recv()
        dcopies.append(send(vpack.at[source, k], vpack.at[source, k], other))
    for copy in dcopies:
        copy.wait_recv()
    full = jnp.concatenate([vpack[z, c] for z in range(4) for c in range(2)], axis=0)
    vsend[...] = jnp.dot(vrow[...], full, preferred_element_type=F32).astype(BF16).reshape(BINS, 96, 256)
    xcopies = [send(vsend.at[o], vrecv.at[x], device(x=o)) for o in xs]
    vrecv[x] = vsend[x]

    wide = lax.broadcasted_iota(jnp.int32, (TILE, 1536), 1) - lax.broadcasted_iota(jnp.int32, (TILE, 1536), 0)
    for h in range(2):
        offset = (zh if h == 0 else 1 - zh) * BIN
        for i in range(TILES):
            pick[h, pl.ds(i * TILE, TILE), :] = jnp.where(wide == bins[i] * HALF + offset + places[i], 1.0, 0.0).astype(BF16)
    for j in range(CHUNKS):
        own_copies[j].wait_recv()
        tpart[j] = jnp.dot(traw[0, j], pick[0], preferred_element_type=F32).astype(BF16)

    for copy in xcopies:
        copy.wait_recv()
    myrows = pl.ds(vmine, 96)
    for h in range(2):
        a, b = vrecv[2 * h], vrecv[2 * h + 1]
        vall[y, myrows, pl.ds(h * HALF, 128)] = a[:, 0:128]
        vall[y, myrows, pl.ds(h * HALF + 128, 128)] = a[:, 128:256] + b[:, 0:128]
        vall[y, myrows, pl.ds(h * HALF + 256, 128)] = b[:, 128:256]
    vcore = [send(vall.at[y, myrows], vall.at[y, myrows], other)]
    ups = [send(vall.at[y, myrows], vall.at[y, myrows], device(y=up))]
    downs = [send(vall.at[y, myrows], vall.at[y, myrows], device(y=down))]

    for i in range(TILES):
        unpick_at = lax.broadcasted_iota(jnp.int32, (256, NVIR), 0)
    for m in range(BINS):
        unpick[pl.ds(m * 256, 256), :] = jnp.where(unpick_at + m * 256 == opad, 1.0, 0.0).astype(BF16)
    osend[...] = jnp.zeros_like(osend)

    tcopies = []

    def regroup(j):
        for copy in far_copies[j]:
            copy.wait_recv()
        tsend[j] = tpart[j] + jnp.dot(traw[1, j], pick[1], preferred_element_type=F32).astype(BF16)
        tcopies.append([
            send(tsend.at[j, :, pl.ds(pl.multiple_of(o * HALF, HALF), HALF)],
                 trecv.at[j, :, pl.ds(pl.multiple_of(x * HALF, HALF), HALF)], device(x=o))
            for o in xs
        ])
        own = pl.ds(pl.multiple_of(x * HALF, HALF), HALF)
        trecv[j, :, own] = tsend[j, :, own]

    for step in range(1, 5):
        from_down, from_up = (y + 8 - step) % 8, (y + step) % 8
        regroup(step - 1)
        if step < 4:
            a, b = vall.at[from_down, myrows], vall.at[from_up, myrows]
            ups[-1].wait_recv()
            if step < 3:
                ups.append(send(a, a, device(y=up)))
            else:
                a_half = vall.at[from_down, pl.ds(vmine, 48)]
                ups.append(send(a_half, a_half, device(y=up)))
            vcore.append(send(a, a, other))
            downs[-1].wait_recv()
            if step < 3:
                downs.append(send(b, b, device(y=down)))
            else:
                b_half = vall.at[from_up, pl.ds(vmine + 48, 48)]
                downs.append(send(b_half, b_half, device(y=down)))
            vcore.append(send(b, b, other))
        else:
            ups[-1].wait_recv()
            downs[-1].wait_recv()
            last = vall.at[from_down, myrows]
            vcore.append(send(last, last, other))
    for copy in vcore:
        copy.wait_recv()

    ocopies = []
    for j in range(CHUNKS):
        for copy in tcopies[j]:
            copy.wait_recv()
        total = jnp.dot(trecv[j], vall[...].reshape(8 * BIN, NVIR), preferred_element_type=F32)
        for a in range(4):
            osend[j, :, pl.ds(a * 256, BIN)] = total[:, a * BIN:(a + 1) * BIN].astype(BF16)
        ocopies.append([
            send(osend.at[j, :, pl.ds(pl.multiple_of(o * 256, 256), 256)],
                 orecv.at[j, :, pl.ds(pl.multiple_of(x * 256, 256), 256)], device(x=o))
            for o in xs
        ])
        own = pl.ds(pl.multiple_of(x * 256, 256), 256)
        orecv[j, :, own] = osend[j, :, own]
    last_copies, locals_ = [], []
    for j in range(CHUNKS):
        for copy in ocopies[j]:
            copy.wait_recv()
        ofull[j] = jnp.dot(orecv[j], unpick[...], preferred_element_type=F32).astype(BF16)
        rows = pl.ds(tmine + j * RC, RC)
        last_copies.append(send(ofull.at[j, :, pl.ds(theirs, HALF)], out_ref.at[rows, :], other))
        local = pltpu.make_async_copy(ofull.at[j, :, pl.ds(mine, HALF)], out_ref.at[rows, :], local_sem.at[j])
        local.start()
        locals_.append(local)
    for copy in last_copies:
        copy.wait_recv()
    for copy in locals_:
        copy.wait()
    for copy in sent:
        copy.wait_send()


SEMS = 80


def binned(amplitudes, integrals, irreps):
    vmem = lambda *shape: pltpu.VMEM(shape, BF16)
    return pl.pallas_call(
        kernel,
        out_shape=jax.ShapeDtypeStruct((512, HALF), BF16),
        in_specs=[
            pl.BlockSpec(memory_space=pltpu.VMEM), pl.BlockSpec(memory_space=pltpu.VMEM),
            pl.BlockSpec(memory_space=pltpu.SMEM),
        ],
        out_specs=pl.BlockSpec(memory_space=pl.ANY),
        scratch_shapes=[
            vmem(2, CHUNKS, RC, NVIR), vmem(CHUNKS, RC, 1536), vmem(CHUNKS, RC, 1536), vmem(CHUNKS, RC, 1536),
            vmem(96, NVIR), vmem(4, 2, 96, 256), vmem(BINS, 96, 256), vmem(4, 96, 256), vmem(8, BIN, NVIR),
            vmem(CHUNKS, RC, 1024), vmem(CHUNKS, RC, 1024), vmem(CHUNKS, RC, NVIR),
            vmem(2, NVIR, 1536), vmem(NVIR, 1024), vmem(HALF, NVIR), vmem(1024, NVIR),
            pltpu.SemaphoreType.DMA((SEMS,)), pltpu.SemaphoreType.DMA((SEMS,)), pltpu.SemaphoreType.DMA((CHUNKS,)),
        ],
        compiler_params=pltpu.CompilerParams(collective_id=0, has_side_effects=True, vmem_limit_bytes=48 << 20),
        name="ladder",
    )(amplitudes, integrals, irreps)


def gathered(amplitudes, integrals, irreps):
    col_first = (lax.axis_index("virt") % 2) * HALF
    col_sym = lax.dynamic_slice_in_dim(irreps, col_first, HALF, 0)
    row_sym = jnp.tile(irreps, 8)
    every = lax.all_gather(amplitudes, "virt", axis=1, tiled=True)
    slab = lax.all_gather(integrals, "pair", axis=0, tiled=True)
    masked = jnp.where(row_sym[:, None] == col_sym[None, :], slab, jnp.zeros_like(slab))
    return jnp.dot(every, masked, preferred_element_type=F32).astype(BF16)


def per_device(amplitudes, integrals, irreps):
    tiles = irreps.reshape(TILES, TILE)[:, 0]
    wide = jnp.any(tiles[:-3] == tiles[3:])
    return lax.cond(wide, gathered, binned, amplitudes, integrals, irreps)


def solution(mesh):
    placed = (P("pair", "virt"), P("pair", "virt"), P())
    return jax.shard_map(
        per_device, mesh=mesh, in_specs=placed, out_specs=P("pair", "virt"), check_vma=False
    )
```

```python
import functools

import jax
import jax.numpy as jnp
from jax import lax
from jax.experimental import pallas as pl
from jax.experimental.pallas import tpu as pltpu
from jax.sharding import PartitionSpec as P

MESH = pl.DeviceIdType.MESH
BF16 = jnp.bfloat16
F32 = jnp.float32
TILE = 64
TILES = 12
BINS = 4
NVIR = 768
HALF = 384
CHUNKS = 4
ROWS = 256
RC = ROWS // CHUNKS
SEMS = 80


def places_of_tiles(irreps_ref):
    irrep = [irreps_ref[TILE * i] for i in range(TILES)]
    count = [sum((irrep[i] == g).astype(jnp.int32) for i in range(TILES)) for g in range(8)]
    big = [(c >= 3).astype(jnp.int32) for c in count]
    two = [(c == 2).astype(jnp.int32) for c in count]
    one = [(c == 1).astype(jnp.int32) for c in count]
    n3, n2 = sum(big), sum(two)
    bins, places = [jnp.int32(0)] * TILES, [jnp.int32(0)] * TILES
    start = r3 = r2 = r1 = jnp.int32(0)
    for g in range(8):
        lone = jnp.where(r1 < n2, 3 * (n3 + r1) + 2, 3 * (n3 + n2) + r1 - n2)
        base = jnp.where(big[g] == 1, 3 * r3, jnp.where(two[g] == 1, 3 * (n3 + r2), lone))
        for i in range(TILES):
            here = irrep[i] == g
            bins[i] = jnp.where(here, base // 3, bins[i])
            places[i] = jnp.where(here, (base % 3 + i - start) * TILE, places[i])
        start, r3, r2, r1 = start + count[g], r3 + big[g], r2 + two[g], r1 + one[g]
    return irrep, bins, places


def kernel(
    W, t_ref, v_ref, irreps_ref, out_ref,
    traw, tpart, tsend, trecv, vraw, vpack, vsend, vrecv, vall, osend, orecv, ofull,
    pick, vpick, vrow, unpick,
    send_sem, recv_sem, local_sem,
):
    PW, W2, H = W + 64, 2 * W, W // 2
    pair, virt = lax.axis_index("pair"), lax.axis_index("virt")
    y, zl = pair // 4, pair % 4
    x, zh, k = virt // 4, (virt // 2) % 2, virt % 2

    def device(x=x, y=y, zh=zh, zl=zl, k=k):
        return (y * 4 + zl, (x * 2 + zh) * 2 + k)

    near = x + 1 - 2 * (x % 2)
    own2, far2 = x // 2, 1 - x // 2
    xs = [(x + j) % 4 for j in (1, 3, 2)]
    zs = [(zl + j) % 4 for j in (1, 2, 3)]
    up, down = (y + 1) % 8, (y + 7) % 8
    peers = (
        [device(k=1 - k), device(zh=1 - zh), device(zh=1 - zh, k=1 - k)]
        + [device(x=o) for o in xs] + [device(zl=o) for o in zs] + [device(y=up), device(y=down)]
    )
    barrier = pltpu.get_barrier_semaphore()
    for peer in peers:
        pl.semaphore_signal(barrier, inc=1, device_id=peer, device_id_type=MESH)

    mine = pl.multiple_of(k * HALF, HALF)
    theirs = pl.multiple_of((1 - k) * HALF, HALF)
    vmine, vtheirs = pl.multiple_of(k * 96, 32), pl.multiple_of((1 - k) * 96, 32)
    tmine, ttheirs = pl.multiple_of(k * ROWS, ROWS), pl.multiple_of((1 - k) * ROWS, ROWS)
    other = device(k=1 - k)

    vown = pltpu.make_async_copy(v_ref.at[pl.ds(vmine, 96), :], vraw.at[:, pl.ds(mine, HALF)], local_sem.at[0])
    vown.start()
    town = pltpu.make_async_copy(t_ref.at[pl.ds(tmine, ROWS), :], traw.at[0, :, pl.ds(mine, HALF)], local_sem.at[1])
    town.start()

    irrep, bins, places = places_of_tiles(irreps_ref)
    shift = (x % 2) * TILE
    padded = [bins[i] * PW + shift + places[i] for i in range(TILES)]

    diff = lax.broadcasted_iota(jnp.int32, (TILE, 4 * PW), 1) - lax.broadcasted_iota(jnp.int32, (TILE, 4 * PW), 0)
    for i in range(TILES):
        vpick[pl.ds(i * TILE, TILE), :] = jnp.where(diff == padded[i], 1.0, 0.0).astype(BF16)
    lane = lax.broadcasted_iota(jnp.int32, (1, 4 * PW), 1)
    lane_irrep = jnp.full((1, 4 * PW), -1, jnp.int32)
    for i in range(TILES):
        lane_irrep = jnp.where((lane >= padded[i]) & (lane < padded[i] + TILE), irrep[i], lane_irrep)

    pl.semaphore_wait(barrier, len(peers))

    used = [0]
    sent = []

    def send(src, dst, to):
        n = used[0]
        used[0] += 1
        copy = pltpu.make_async_remote_copy(
            src_ref=src, dst_ref=dst, send_sem=send_sem.at[n], recv_sem=recv_sem.at[n],
            device_id=to, device_id_type=MESH,
        )
        copy.start()
        sent.append(copy)
        return copy

    far_copies = []

    def send_far(j):
        lanes = pl.ds(mine, HALF)
        dst = traw.at[1, pl.ds(j * RC, RC), lanes]
        far_copies.append([
            send(t_ref.at[pl.ds(tmine + j * RC, RC), :], dst, device(zh=1 - zh)),
            send(t_ref.at[pl.ds(ttheirs + j * RC, RC), :], dst, device(zh=1 - zh, k=1 - k)),
        ])

    vraw_copy = send(v_ref.at[pl.ds(vtheirs, 96), :], vraw.at[:, pl.ds(mine, HALF)], other)
    send_far(0)
    traw_copy = send(t_ref.at[pl.ds(ttheirs, ROWS), :], traw.at[0, :, pl.ds(mine, HALF)], other)

    vown.wait()
    vraw_copy.wait_recv()
    packed = jnp.dot(vraw[...], vpick[...], preferred_element_type=F32)
    for j in range(3):
        row_irrep = irreps_ref[TILE * (3 * zl + (k * 3 + j) // 2)]
        part = jnp.where(lane_irrep == row_irrep, packed[j * 32:(j + 1) * 32, :], 0.0)
        part = part[:, 0:PW] + part[:, PW:2 * PW] + part[:, 2 * PW:3 * PW] + part[:, 3 * PW:4 * PW]
        vpack[zl, k, pl.ds(j * 32, 32), :] = part.astype(BF16)
    mypack = vpack.at[zl, k]
    zcopies = [send(mypack, mypack, device(zl=o)) for o in zs]
    dcopies = [send(mypack, mypack, other)]
    for j in range(1, CHUNKS):
        send_far(j)

    olane = lax.broadcasted_iota(jnp.int32, (1, NVIR), 1)
    oslot = jnp.zeros((1, NVIR), jnp.int32)
    opad = jnp.zeros((1, NVIR), jnp.int32)
    for i in range(TILES):
        here = (olane >= i * TILE) & (olane < (i + 1) * TILE)
        oslot = jnp.where(here, bins[i] * W + places[i] + olane - i * TILE, oslot)
        opad = jnp.where(here, padded[i] + olane - i * TILE, opad)
    for m in range(BINS):
        want = lax.broadcasted_iota(jnp.int32, (H, NVIR), 0) + m * W + k * H
        vrow[pl.ds(m * H, H), :] = jnp.where(want == oslot, 1.0, 0.0).astype(BF16)

    wide = lax.broadcasted_iota(jnp.int32, (TILE, 4 * W2), 1) - lax.broadcasted_iota(jnp.int32, (TILE, 4 * W2), 0)
    for h in range(2):
        offset = (zh if h == 0 else 1 - zh) * W
        for i in range(TILES):
            pick[h, pl.ds(i * TILE, TILE), :] = jnp.where(wide == bins[i] * W2 + offset + places[i], 1.0, 0.0).astype(BF16)

    for j, o in enumerate(zs):
        source = (zl + 4 - (1, 2, 3)[j]) % 4
        zcopies[j].wait_recv()
        dcopies.append(send(vpack.at[source, k], vpack.at[source, k], other))

    town.wait()
    traw_copy.wait_recv()
    tpart[...] = jnp.dot(traw[0], pick[0], preferred_element_type=F32).astype(BF16)

    for copy in dcopies:
        copy.wait_recv()
    full = jnp.concatenate([vpack[z, c] for z in range(4) for c in range(2)], axis=0)
    vsend[...] = jnp.dot(vrow[...], full, preferred_element_type=F32).astype(BF16).reshape(BINS, H, PW)
    xcopies = [send(vsend.at[o], vrecv.at[x], device(x=o)) for o in xs]
    vrecv[x] = vsend[x]

    tcopies = []

    def regroup(j):
        rows = pl.ds(j * RC, RC)
        for copy in far_copies[j]:
            copy.wait_recv()
        tsend[rows, :] = tpart[rows, :] + jnp.dot(traw[1, rows, :], pick[1], preferred_element_type=F32).astype(BF16)
        own = pl.ds(pl.multiple_of(x * W2, W2), W2)
        tcopies.append([
            send(tsend.at[rows, pl.ds(pl.multiple_of(o * W2, W2), W2)], trecv.at[rows, own], device(x=o)) for o in xs
        ])
        trecv[rows, own] = tsend[rows, own]

    regroup(0)

    for copy in xcopies:
        copy.wait_recv()
    myrows = pl.ds(pl.multiple_of(k * H, 16), H)
    pairs = [pl.ds(pl.multiple_of(p * W2, W2), W2) for p in (far2, own2)]
    vcore, ups, downs = [], [[], []], [[], []]

    def share(ref):
        vcore.append(send(ref, ref, other))

    for p, q in enumerate((far2, own2)):
        a, b = vrecv[2 * q], vrecv[2 * q + 1]
        merged = jnp.concatenate([a[:, :W - 64], a[:, W - 64:] + b[:, :128], b[:, 128:]], axis=1)
        vall[y, myrows, pairs[p]] = merged
        piece = vall.at[y, myrows, pairs[p]]
        ups[p].append(send(piece, piece, device(y=up)))
        downs[p].append(send(piece, piece, device(y=down)))
        share(piece)

    unpick_at = lax.broadcasted_iota(jnp.int32, (PW, NVIR), 0)
    for m in range(BINS):
        unpick[pl.ds(m * PW, PW), :] = jnp.where(unpick_at + m * PW == opad, 1.0, 0.0).astype(BF16)

    regroup(1)

    def relay(step, p):
        from_down, from_up = (y + 8 - step) % 8, (y + step) % 8
        a, b = vall.at[from_down, myrows, pairs[p]], vall.at[from_up, myrows, pairs[p]]
        ups[p][-1].wait_recv()
        if step == 4:
            downs[p][-1].wait_recv()
            share(a)
            return
        if step < 3:
            ups[p].append(send(a, a, device(y=up)))
        else:
            half = vall.at[from_down, pl.ds(pl.multiple_of(k * H, 16), H // 2), pairs[p]]
            ups[p].append(send(half, half, device(y=up)))
        downs[p][-1].wait_recv()
        if step < 3:
            downs[p].append(send(b, b, device(y=down)))
        else:
            half = vall.at[from_up, pl.ds(pl.multiple_of(k * H + H // 2, 16), H // 2), pairs[p]]
            downs[p].append(send(half, half, device(y=down)))
        share(a)
        share(b)

    relay(1, 0)
    relay(1, 1)
    regroup(2)
    relay(2, 0)
    relay(2, 1)
    regroup(3)
    relay(3, 0)
    relay(3, 1)
    relay(4, 0)
    for copies in tcopies:
        for copy in copies:
            copy.wait_recv()

    ocopies = []
    into = pl.ds(pl.multiple_of(x * PW, 128), PW)

    def multiply(p):
        while vcore and vcore[0] is not None:
            vcore.pop(0).wait_recv()
        total = jnp.dot(trecv[...], vall[:, :, pairs[p]].reshape(8 * W, W2), preferred_element_type=F32)
        osend[p] = total.astype(BF16)

    same = pl.multiple_of((x % 2) * (W2 - PW), 128)
    swap = pl.multiple_of((1 - x % 2) * (W2 - PW), 128)
    multiply(0)
    ocopies.append(send(osend.at[0, :, pl.ds(same, PW)], orecv.at[:, into], device(x=2 * far2 + x % 2)))
    ocopies.append(send(osend.at[0, :, pl.ds(swap, PW)], orecv.at[:, into], device(x=2 * far2 + 1 - x % 2)))
    relay(4, 1)
    multiply(1)
    halves = []
    for h in range(2):
        rows = pl.ds(h * 128, 128)
        halves.append(send(osend.at[1, rows, pl.ds(swap, PW)], orecv.at[rows, into], device(x=near)))
    orecv[:, into] = osend[1, :, pl.ds(same, PW)]
    for copy in ocopies:
        copy.wait_recv()
    last, locals_ = [], []
    for h in range(2):
        rows = pl.ds(h * 128, 128)
        halves[h].wait_recv()
        ofull[rows, :] = jnp.dot(orecv[rows, :], unpick[...], preferred_element_type=F32).astype(BF16)
        to = pl.ds(tmine + h * 128, 128)
        last.append(send(ofull.at[rows, pl.ds(theirs, HALF)], out_ref.at[to, :], other))
        local = pltpu.make_async_copy(ofull.at[rows, pl.ds(mine, HALF)], out_ref.at[to, :], local_sem.at[2 + h])
        local.start()
        locals_.append(local)
    for copy in last:
        copy.wait_recv()
    for copy in locals_:
        copy.wait()
    for copy in sent:
        copy.wait_send()


def ladder(width, amplitudes, integrals, irreps):
    vmem = lambda *shape: pltpu.VMEM(shape, BF16)
    W, PW, W2, H = width, width + 64, 2 * width, width // 2
    return pl.pallas_call(
        functools.partial(kernel, W),
        out_shape=jax.ShapeDtypeStruct((512, HALF), BF16),
        in_specs=[
            pl.BlockSpec(memory_space=pl.ANY), pl.BlockSpec(memory_space=pl.ANY),
            pl.BlockSpec(memory_space=pltpu.SMEM),
        ],
        out_specs=pl.BlockSpec(memory_space=pl.ANY),
        scratch_shapes=[
            vmem(2, ROWS, NVIR), vmem(ROWS, 4 * W2), vmem(ROWS, 4 * W2), vmem(ROWS, 4 * W2),
            vmem(96, NVIR), vmem(4, 2, 96, PW), vmem(BINS, H, PW), vmem(4, H, PW), vmem(8, W, 4 * W),
            vmem(2, ROWS, W2), vmem(ROWS, 4 * PW), vmem(ROWS, NVIR),
            vmem(2, NVIR, 4 * W2), vmem(NVIR, 4 * PW), vmem(4 * H, NVIR), vmem(4 * PW, NVIR),
            pltpu.SemaphoreType.DMA((SEMS,)), pltpu.SemaphoreType.DMA((SEMS,)), pltpu.SemaphoreType.DMA((4,)),
        ],
        compiler_params=pltpu.CompilerParams(
            collective_id=width // 300, has_side_effects=True, vmem_limit_bytes=56 << 20
        ),
        name="ladder%d" % width,
    )(amplitudes, integrals, irreps)


def per_device(amplitudes, integrals, irreps):
    wide = jnp.any(irreps[:-192] == irreps[192:])
    return lax.cond(
        wide, functools.partial(ladder, 320), functools.partial(ladder, 192), amplitudes, integrals, irreps
    )


def solution(mesh):
    placed = (P("pair", "virt"), P("pair", "virt"), P())
    return jax.shard_map(
        per_device, mesh=mesh, in_specs=placed, out_specs=P("pair", "virt"), check_vma=False
    )
```

```python
import functools

import jax
import jax.numpy as jnp
from jax import lax
from jax.experimental import pallas as pl
from jax.experimental.pallas import tpu as pltpu
from jax.sharding import PartitionSpec as P

MESH = pl.DeviceIdType.MESH
BF16 = jnp.bfloat16
F32 = jnp.float32
TILE = 64
TILES = 12
BINS = 4
NVIR = 768
HALF = 384
ROWS = 256
CHUNKS = ((0, 32), (32, 32), (64, 64), (128, 64), (192, 64))
SEMS = 128


def places_of_tiles(irreps_ref):
    irrep = [irreps_ref[TILE * i] for i in range(TILES)]
    count = [sum((irrep[i] == g).astype(jnp.int32) for i in range(TILES)) for g in range(8)]
    big = [(c >= 3).astype(jnp.int32) for c in count]
    two = [(c == 2).astype(jnp.int32) for c in count]
    one = [(c == 1).astype(jnp.int32) for c in count]
    n3, n2 = sum(big), sum(two)
    bins, places = [jnp.int32(0)] * TILES, [jnp.int32(0)] * TILES
    start = r3 = r2 = r1 = jnp.int32(0)
    for g in range(8):
        lone = jnp.where(r1 < n2, 3 * (n3 + r1) + 2, 3 * (n3 + n2) + r1 - n2)
        base = jnp.where(big[g] == 1, 3 * r3, jnp.where(two[g] == 1, 3 * (n3 + r2), lone))
        for i in range(TILES):
            here = irrep[i] == g
            bins[i] = jnp.where(here, base // 3, bins[i])
            places[i] = jnp.where(here, (base % 3 + i - start) * TILE, places[i])
        start, r3, r2, r1 = start + count[g], r3 + big[g], r2 + two[g], r1 + one[g]
    return irrep, bins, places


def kernel(
    W, t_ref, v_ref, irreps_ref, out_ref,
    traw, tpart, tsend, trecv, vraw, vpack, vsend, vrecv, vall, osend, orecv, ofull,
    pick, vpick, vrow, unpick,
    send_sem, recv_sem, local_sem,
):
    PW, W2, H = W + 64, 2 * W, W // 2
    pair, virt = lax.axis_index("pair"), lax.axis_index("virt")
    y, zl = pair // 4, pair % 4
    x, zh, k = virt // 4, (virt // 2) % 2, virt % 2

    def device(x=x, y=y, zh=zh, zl=zl, k=k):
        return (y * 4 + zl, (x * 2 + zh) * 2 + k)

    near = x + 1 - 2 * (x % 2)
    own2, far2 = x // 2, 1 - x // 2
    xs = [(x + j) % 4 for j in (2, 1, 3)]
    zs = [(zl + j) % 4 for j in (1, 2, 3)]
    up, down = (y + 1) % 8, (y + 7) % 8
    peers = (
        [device(k=1 - k), device(zh=1 - zh), device(zh=1 - zh, k=1 - k)]
        + [device(x=o) for o in xs] + [device(zl=o) for o in zs] + [device(y=up), device(y=down)]
    )
    barrier = pltpu.get_barrier_semaphore()
    for peer in peers:
        pl.semaphore_signal(barrier, inc=1, device_id=peer, device_id_type=MESH)

    mine = pl.multiple_of(k * HALF, HALF)
    theirs = pl.multiple_of((1 - k) * HALF, HALF)
    vmine, vtheirs = pl.multiple_of(k * 96, 32), pl.multiple_of((1 - k) * 96, 32)
    tmine, ttheirs = pl.multiple_of(k * ROWS, ROWS), pl.multiple_of((1 - k) * ROWS, ROWS)
    other = device(k=1 - k)

    vown = pltpu.make_async_copy(v_ref.at[pl.ds(vmine, 96), :], vraw.at[:, pl.ds(mine, HALF)], local_sem.at[0])
    vown.start()
    town = pltpu.make_async_copy(t_ref.at[pl.ds(tmine, ROWS), :], traw.at[0, :, pl.ds(mine, HALF)], local_sem.at[1])
    town.start()

    irrep, bins, places = places_of_tiles(irreps_ref)
    shift = (x % 2) * TILE
    padded = [bins[i] * PW + shift + places[i] for i in range(TILES)]

    diff = lax.broadcasted_iota(jnp.int32, (TILE, 4 * PW), 1) - lax.broadcasted_iota(jnp.int32, (TILE, 4 * PW), 0)
    for i in range(TILES):
        vpick[pl.ds(i * TILE, TILE), :] = jnp.where(diff == padded[i], 1.0, 0.0).astype(BF16)
    lane = lax.broadcasted_iota(jnp.int32, (1, 4 * PW), 1)
    lane_irrep = jnp.full((1, 4 * PW), -1, jnp.int32)
    for i in range(TILES):
        lane_irrep = jnp.where((lane >= padded[i]) & (lane < padded[i] + TILE), irrep[i], lane_irrep)

    pl.semaphore_wait(barrier, len(peers))

    used = [0]
    sent = []

    def send(src, dst, to):
        n = used[0]
        used[0] += 1
        copy = pltpu.make_async_remote_copy(
            src_ref=src, dst_ref=dst, send_sem=send_sem.at[n], recv_sem=recv_sem.at[n],
            device_id=to, device_id_type=MESH,
        )
        copy.start()
        sent.append(copy)
        return copy

    far_copies = []

    def send_far(j):
        first, count = CHUNKS[j]
        dst = traw.at[1, pl.ds(first, count), pl.ds(mine, HALF)]
        far_copies.append([
            send(t_ref.at[pl.ds(tmine + first, count), :], dst, device(zh=1 - zh)),
            send(t_ref.at[pl.ds(ttheirs + first, count), :], dst, device(zh=1 - zh, k=1 - k)),
        ])

    vraw_copy = send(v_ref.at[pl.ds(vtheirs, 96), :], vraw.at[:, pl.ds(mine, HALF)], other)
    traw_copy = send(t_ref.at[pl.ds(ttheirs, ROWS), :], traw.at[0, :, pl.ds(mine, HALF)], other)

    vown.wait()
    vraw_copy.wait_recv()
    packed = jnp.dot(vraw[...], vpick[...], preferred_element_type=F32)
    for j in range(3):
        row_irrep = irreps_ref[TILE * (3 * zl + (k * 3 + j) // 2)]
        part = jnp.where(lane_irrep == row_irrep, packed[j * 32:(j + 1) * 32, :], 0.0)
        part = part[:, 0:PW] + part[:, PW:2 * PW] + part[:, 2 * PW:3 * PW] + part[:, 3 * PW:4 * PW]
        vpack[zl, k, pl.ds(j * 32, 32), :] = part.astype(BF16)
    mypack = vpack.at[zl, k]
    zcopies = [send(mypack, mypack, device(zl=o)) for o in zs]
    dcopies = [send(mypack, mypack, other)]

    olane = lax.broadcasted_iota(jnp.int32, (1, NVIR), 1)
    oslot = jnp.zeros((1, NVIR), jnp.int32)
    opad = jnp.zeros((1, NVIR), jnp.int32)
    for i in range(TILES):
        here = (olane >= i * TILE) & (olane < (i + 1) * TILE)
        oslot = jnp.where(here, bins[i] * W + places[i] + olane - i * TILE, oslot)
        opad = jnp.where(here, padded[i] + olane - i * TILE, opad)
    for m in range(BINS):
        want = lax.broadcasted_iota(jnp.int32, (H, NVIR), 0) + m * W + k * H
        vrow[pl.ds(m * H, H), :] = jnp.where(want == oslot, 1.0, 0.0).astype(BF16)

    wide = lax.broadcasted_iota(jnp.int32, (TILE, 4 * W2), 1) - lax.broadcasted_iota(jnp.int32, (TILE, 4 * W2), 0)
    for h in range(2):
        offset = (zh if h == 0 else 1 - zh) * W
        for i in range(TILES):
            pick[h, pl.ds(i * TILE, TILE), :] = jnp.where(wide == bins[i] * W2 + offset + places[i], 1.0, 0.0).astype(BF16)

    for j, o in enumerate(zs):
        source = (zl + 4 - (1, 2, 3)[j]) % 4
        zcopies[j].wait_recv()
        dcopies.append(send(vpack.at[source, k], vpack.at[source, k], other))
    for j in range(len(CHUNKS)):
        send_far(j)

    town.wait()
    traw_copy.wait_recv()
    tpart[...] = jnp.dot(traw[0], pick[0], preferred_element_type=F32).astype(BF16)

    for copy in dcopies:
        copy.wait_recv()
    full = jnp.concatenate([vpack[z, c] for z in range(4) for c in range(2)], axis=0)
    vsend[...] = jnp.dot(vrow[...], full, preferred_element_type=F32).astype(BF16).reshape(BINS, H, PW)
    xcopies = [send(vsend.at[o], vrecv.at[x], device(x=o)) for o in xs]
    vrecv[x] = vsend[x]

    tcopies = []

    def regroup(j):
        rows = pl.ds(*CHUNKS[j])
        for copy in far_copies[j]:
            copy.wait_recv()
        tsend[rows, :] = tpart[rows, :] + jnp.dot(traw[1, rows, :], pick[1], preferred_element_type=F32).astype(BF16)
        own = pl.ds(pl.multiple_of(x * W2, W2), W2)
        tcopies.append([
            send(tsend.at[rows, pl.ds(pl.multiple_of(o * W2, W2), W2)], trecv.at[rows, own], device(x=o)) for o in xs
        ])
        trecv[rows, own] = tsend[rows, own]

    for copy in xcopies:
        copy.wait_recv()
    myrows = pl.ds(pl.multiple_of(k * H, 16), H)
    same = pl.multiple_of((x % 2) * (W2 - PW), 128)
    swap = pl.multiple_of((1 - x % 2) * (W2 - PW), 128)
    far_lane, own_lane = far2 * W2, own2 * W2
    pieces = [
        pl.ds(pl.multiple_of(far_lane, 128), PW),
        pl.ds(pl.multiple_of(far_lane + PW, 128), W2 - PW),
        pl.ds(pl.multiple_of(own_lane + swap, 128), PW),
        pl.ds(pl.multiple_of(own_lane + (x % 2) * PW, 128), W2 - PW),
    ]
    vcore, ups, downs = [[], [], [], []], [[], [], [], []], [[], [], [], []]

    def share(p, ref):
        vcore[p].append(send(ref, ref, other))

    for q in (far2, own2):
        a, b = vrecv[2 * q], vrecv[2 * q + 1]
        merged = jnp.concatenate([a[:, :W - 64], a[:, W - 64:] + b[:, :128], b[:, 128:]], axis=1)
        vall[y, myrows, pl.ds(pl.multiple_of(q * W2, 128), W2)] = merged
    for p in range(4):
        piece = vall.at[y, myrows, pieces[p]]
        ups[p].append(send(piece, piece, device(y=up)))
        downs[p].append(send(piece, piece, device(y=down)))
    for p in range(4):
        share(p, vall.at[y, myrows, pieces[p]])

    unpick_at = lax.broadcasted_iota(jnp.int32, (PW, NVIR), 0)
    for m in range(BINS):
        unpick[pl.ds(m * PW, PW), :] = jnp.where(unpick_at + m * PW == opad, 1.0, 0.0).astype(BF16)

    def relay(step, p):
        from_down, from_up = (y + 8 - step) % 8, (y + step) % 8
        a, b = vall.at[from_down, myrows, pieces[p]], vall.at[from_up, myrows, pieces[p]]
        ups[p][-1].wait_recv()
        if step == 4:
            downs[p][-1].wait_recv()
            share(p, a)
            return
        if step < 3:
            ups[p].append(send(a, a, device(y=up)))
        else:
            half = vall.at[from_down, pl.ds(pl.multiple_of(k * H, 16), H // 2), pieces[p]]
            ups[p].append(send(half, half, device(y=up)))
        downs[p][-1].wait_recv()
        if step < 3:
            downs[p].append(send(b, b, device(y=down)))
        else:
            half = vall.at[from_up, pl.ds(pl.multiple_of(k * H + H // 2, 16), H // 2), pieces[p]]
            downs[p].append(send(half, half, device(y=down)))
        share(p, a)
        share(p, b)

    regroup(0)
    regroup(1)
    for step in range(1, 4):
        for p in range(4):
            relay(step, p)
        regroup(step + 1)
    relay(4, 0)
    relay(4, 1)
    for copies in tcopies:
        for copy in copies:
            copy.wait_recv()

    into = pl.ds(pl.multiple_of(x * PW, 128), PW)

    def multiply(rows, lanes):
        block = vall[:, :, lanes].reshape(8 * W, lanes.size)
        return jnp.dot(trecv[rows, :], block, preferred_element_type=F32).astype(BF16)

    def arrived(*which):
        for p in which:
            for copy in vcore[p]:
                copy.wait_recv()

    arrived(0, 1)
    osend[0] = multiply(pl.ds(0, ROWS), pl.ds(pl.multiple_of(far_lane, 128), W2))
    ocopies = [
        send(osend.at[0, :, pl.ds(same, PW)], orecv.at[:, into], device(x=2 * far2 + x % 2)),
        send(osend.at[0, :, pl.ds(swap, PW)], orecv.at[:, into], device(x=2 * far2 + 1 - x % 2)),
    ]
    relay(4, 2)
    relay(4, 3)
    arrived(2)
    halves = []
    for h in range(2):
        rows = pl.ds(h * 128, 128)
        osend[1, rows, pl.ds(0, PW)] = multiply(rows, pieces[2])
        halves.append(send(osend.at[1, rows, pl.ds(0, PW)], orecv.at[rows, into], device(x=near)))
    arrived(3)
    orecv[:, into] = multiply(pl.ds(0, ROWS), pl.ds(pl.multiple_of(own_lane + same, 128), PW))
    for copy in ocopies:
        copy.wait_recv()
    last, locals_ = [], []
    for h in range(2):
        rows = pl.ds(h * 128, 128)
        halves[h].wait_recv()
        ofull[rows, :] = jnp.dot(orecv[rows, :], unpick[...], preferred_element_type=F32).astype(BF16)
        to = pl.ds(tmine + h * 128, 128)
        last.append(send(ofull.at[rows, pl.ds(theirs, HALF)], out_ref.at[to, :], other))
        local = pltpu.make_async_copy(ofull.at[rows, pl.ds(mine, HALF)], out_ref.at[to, :], local_sem.at[2 + h])
        local.start()
        locals_.append(local)
    for copy in last:
        copy.wait_recv()
    for copy in locals_:
        copy.wait()
    for copy in sent:
        copy.wait_send()


def ladder(width, amplitudes, integrals, irreps):
    vmem = lambda *shape: pltpu.VMEM(shape, BF16)
    W, PW, W2, H = width, width + 64, 2 * width, width // 2
    return pl.pallas_call(
        functools.partial(kernel, W),
        out_shape=jax.ShapeDtypeStruct((512, HALF), BF16),
        in_specs=[
            pl.BlockSpec(memory_space=pl.ANY), pl.BlockSpec(memory_space=pl.ANY),
            pl.BlockSpec(memory_space=pltpu.SMEM),
        ],
        out_specs=pl.BlockSpec(memory_space=pl.ANY),
        scratch_shapes=[
            vmem(2, ROWS, NVIR), vmem(ROWS, 4 * W2), vmem(ROWS, 4 * W2), vmem(ROWS, 4 * W2),
            vmem(96, NVIR), vmem(4, 2, 96, PW), vmem(BINS, H, PW), vmem(4, H, PW), vmem(8, W, 4 * W),
            vmem(2, ROWS, W2), vmem(ROWS, 4 * PW), vmem(ROWS, NVIR),
            vmem(2, NVIR, 4 * W2), vmem(NVIR, 4 * PW), vmem(4 * H, NVIR), vmem(4 * PW, NVIR),
            pltpu.SemaphoreType.DMA((SEMS,)), pltpu.SemaphoreType.DMA((SEMS,)), pltpu.SemaphoreType.DMA((4,)),
        ],
        compiler_params=pltpu.CompilerParams(
            collective_id=width // 300, has_side_effects=True, vmem_limit_bytes=56 << 20
        ),
        name="ladder%d" % width,
    )(amplitudes, integrals, irreps)


def per_device(amplitudes, integrals, irreps):
    wide = jnp.any(irreps[:-192] == irreps[192:])
    return lax.cond(
        wide, functools.partial(ladder, 320), functools.partial(ladder, 192), amplitudes, integrals, irreps
    )


def solution(mesh):
    placed = (P("pair", "virt"), P("pair", "virt"), P())
    return jax.shard_map(
        per_device, mesh=mesh, in_specs=placed, out_specs=P("pair", "virt"), check_vma=False
    )
```

```python
import functools

import jax
import jax.numpy as jnp
from jax import lax
from jax.experimental import pallas as pl
from jax.experimental.pallas import tpu as pltpu
from jax.sharding import PartitionSpec as P

MESH = pl.DeviceIdType.MESH
BF16 = jnp.bfloat16
F32 = jnp.float32
TILE = 64
TILES = 12
BINS = 4
NVIR = 768
HALF = 384
ROWS = 256
CHUNKS = ((0, 32), (32, 32), (64, 64), (128, 64), (192, 64))
SEMS = 128


def places_of_tiles(irreps_ref):
    irrep = [irreps_ref[TILE * i] for i in range(TILES)]
    count = [sum((irrep[i] == g).astype(jnp.int32) for i in range(TILES)) for g in range(8)]
    big = [(c >= 3).astype(jnp.int32) for c in count]
    two = [(c == 2).astype(jnp.int32) for c in count]
    one = [(c == 1).astype(jnp.int32) for c in count]
    n3, n2 = sum(big), sum(two)
    bins, places = [jnp.int32(0)] * TILES, [jnp.int32(0)] * TILES
    start = r3 = r2 = r1 = jnp.int32(0)
    for g in range(8):
        lone = jnp.where(r1 < n2, 3 * (n3 + r1) + 2, 3 * (n3 + n2) + r1 - n2)
        base = jnp.where(big[g] == 1, 3 * r3, jnp.where(two[g] == 1, 3 * (n3 + r2), lone))
        for i in range(TILES):
            here = irrep[i] == g
            bins[i] = jnp.where(here, base // 3, bins[i])
            places[i] = jnp.where(here, (base % 3 + i - start) * TILE, places[i])
        start, r3, r2, r1 = start + count[g], r3 + big[g], r2 + two[g], r1 + one[g]
    return irrep, bins, places


def kernel(
    W, t_ref, v_ref, irreps_ref, out_ref,
    traw, tpart, tsend, trecv, vraw, vpack, vsend, vrecv, vall, osend, orecv, ofull,
    pick, vpick, vrow, unpick,
    send_sem, recv_sem, local_sem,
):
    PW, W2, H = W + 64, 2 * W, W // 2
    pair, virt = lax.axis_index("pair"), lax.axis_index("virt")
    y, zl = pair // 4, pair % 4
    x, zh, k = virt // 4, (virt // 2) % 2, virt % 2

    def device(x=x, y=y, zh=zh, zl=zl, k=k):
        return (y * 4 + zl, (x * 2 + zh) * 2 + k)

    near = x + 1 - 2 * (x % 2)
    own2, far2 = x // 2, 1 - x // 2
    xs = [(x + j) % 4 for j in (2, 1, 3)]
    zs = [(zl + j) % 4 for j in (1, 2, 3)]
    up, down = (y + 1) % 8, (y + 7) % 8
    peers = (
        [device(k=1 - k), device(zh=1 - zh), device(zh=1 - zh, k=1 - k)]
        + [device(x=o) for o in xs] + [device(zl=o) for o in zs] + [device(y=up), device(y=down)]
    )
    barrier = pltpu.get_barrier_semaphore()
    for peer in peers:
        pl.semaphore_signal(barrier, inc=1, device_id=peer, device_id_type=MESH)

    mine = pl.multiple_of(k * HALF, HALF)
    theirs = pl.multiple_of((1 - k) * HALF, HALF)
    vmine, vtheirs = pl.multiple_of(k * 96, 32), pl.multiple_of((1 - k) * 96, 32)
    tmine, ttheirs = pl.multiple_of(k * ROWS, ROWS), pl.multiple_of((1 - k) * ROWS, ROWS)
    other = device(k=1 - k)

    vown = pltpu.make_async_copy(v_ref.at[pl.ds(vmine, 96), :], vraw.at[:, pl.ds(mine, HALF)], local_sem.at[0])
    vown.start()
    town = pltpu.make_async_copy(t_ref.at[pl.ds(tmine, ROWS), :], traw.at[0, :, pl.ds(mine, HALF)], local_sem.at[1])
    town.start()

    irrep, bins, places = places_of_tiles(irreps_ref)
    shift = (x % 2) * TILE
    padded = [bins[i] * PW + shift + places[i] for i in range(TILES)]

    diff = lax.broadcasted_iota(jnp.int32, (TILE, 4 * PW), 1) - lax.broadcasted_iota(jnp.int32, (TILE, 4 * PW), 0)
    for i in range(TILES):
        vpick[pl.ds(i * TILE, TILE), :] = jnp.where(diff == padded[i], 1.0, 0.0).astype(BF16)
    lane = lax.broadcasted_iota(jnp.int32, (1, 4 * PW), 1)
    lane_irrep = jnp.full((1, 4 * PW), -1, jnp.int32)
    for i in range(TILES):
        lane_irrep = jnp.where((lane >= padded[i]) & (lane < padded[i] + TILE), irrep[i], lane_irrep)

    pl.semaphore_wait(barrier, len(peers))

    used = [0]
    sent = []

    def send(src, dst, to):
        n = used[0]
        used[0] += 1
        copy = pltpu.make_async_remote_copy(
            src_ref=src, dst_ref=dst, send_sem=send_sem.at[n], recv_sem=recv_sem.at[n],
            device_id=to, device_id_type=MESH,
        )
        copy.start()
        sent.append(copy)
        return copy

    far_copies = []

    def send_far(j):
        first, count = CHUNKS[j]
        dst = traw.at[1, pl.ds(first, count), pl.ds(mine, HALF)]
        far_copies.append([
            send(t_ref.at[pl.ds(tmine + first, count), :], dst, device(zh=1 - zh)),
            send(t_ref.at[pl.ds(ttheirs + first, count), :], dst, device(zh=1 - zh, k=1 - k)),
        ])

    vraw_copy = send(v_ref.at[pl.ds(vtheirs, 96), :], vraw.at[:, pl.ds(mine, HALF)], other)
    traw_copy = send(t_ref.at[pl.ds(ttheirs, ROWS), :], traw.at[0, :, pl.ds(mine, HALF)], other)

    vown.wait()
    vraw_copy.wait_recv()
    packed = jnp.dot(vraw[...], vpick[...], preferred_element_type=F32)
    for j in range(3):
        row_irrep = irreps_ref[TILE * (3 * zl + (k * 3 + j) // 2)]
        part = jnp.where(lane_irrep == row_irrep, packed[j * 32:(j + 1) * 32, :], 0.0)
        part = part[:, 0:PW] + part[:, PW:2 * PW] + part[:, 2 * PW:3 * PW] + part[:, 3 * PW:4 * PW]
        vpack[zl, k, pl.ds(j * 32, 32), :] = part.astype(BF16)
    mypack = vpack.at[zl, k]
    zcopies = [send(mypack, mypack, device(zl=o)) for o in zs]
    dcopies = [send(mypack, mypack, other)]

    olane = lax.broadcasted_iota(jnp.int32, (1, NVIR), 1)
    oslot = jnp.zeros((1, NVIR), jnp.int32)
    opad = jnp.zeros((1, NVIR), jnp.int32)
    for i in range(TILES):
        here = (olane >= i * TILE) & (olane < (i + 1) * TILE)
        oslot = jnp.where(here, bins[i] * W + places[i] + olane - i * TILE, oslot)
        opad = jnp.where(here, padded[i] + olane - i * TILE, opad)
    for m in range(BINS):
        want = lax.broadcasted_iota(jnp.int32, (H, NVIR), 0) + m * W + k * H
        vrow[pl.ds(m * H, H), :] = jnp.where(want == oslot, 1.0, 0.0).astype(BF16)

    wide = lax.broadcasted_iota(jnp.int32, (TILE, 4 * W2), 1) - lax.broadcasted_iota(jnp.int32, (TILE, 4 * W2), 0)
    for h in range(2):
        offset = (zh if h == 0 else 1 - zh) * W
        for i in range(TILES):
            pick[h, pl.ds(i * TILE, TILE), :] = jnp.where(wide == bins[i] * W2 + offset + places[i], 1.0, 0.0).astype(BF16)

    for j, o in enumerate(zs):
        source = (zl + 4 - (1, 2, 3)[j]) % 4
        zcopies[j].wait_recv()
        dcopies.append(send(vpack.at[source, k], vpack.at[source, k], other))
    for j in range(len(CHUNKS)):
        send_far(j)

    town.wait()
    traw_copy.wait_recv()
    tpart[...] = jnp.dot(traw[0], pick[0], preferred_element_type=F32).astype(BF16)

    for copy in dcopies:
        copy.wait_recv()
    full = jnp.concatenate([vpack[z, c] for z in range(4) for c in range(2)], axis=0)
    vsend[...] = jnp.dot(vrow[...], full, preferred_element_type=F32).astype(BF16).reshape(BINS, H, PW)
    xcopies = [send(vsend.at[o], vrecv.at[x], device(x=o)) for o in xs]
    vrecv[x] = vsend[x]

    tcopies = []

    def regroup(j):
        rows = pl.ds(*CHUNKS[j])
        for copy in far_copies[j]:
            copy.wait_recv()
        tsend[rows, :] = tpart[rows, :] + jnp.dot(traw[1, rows, :], pick[1], preferred_element_type=F32).astype(BF16)
        own = pl.ds(pl.multiple_of(x * W2, W2), W2)
        tcopies.append([
            send(tsend.at[rows, pl.ds(pl.multiple_of(o * W2, W2), W2)], trecv.at[rows, own], device(x=o)) for o in xs
        ])
        trecv[rows, own] = tsend[rows, own]

    for copy in xcopies:
        copy.wait_recv()
    myrows = pl.ds(pl.multiple_of(k * H, 16), H)
    same = pl.multiple_of((x % 2) * (W2 - PW), 128)
    swap = pl.multiple_of((1 - x % 2) * (W2 - PW), 128)
    far_lane, own_lane = far2 * W2, own2 * W2
    pieces = [
        pl.ds(pl.multiple_of(far_lane, 128), PW),
        pl.ds(pl.multiple_of(far_lane + PW, 128), W2 - PW),
        pl.ds(pl.multiple_of(own_lane + swap, 128), PW),
        pl.ds(pl.multiple_of(own_lane + (x % 2) * PW, 128), W2 - PW),
    ]
    vcore, ups, downs = [[], [], [], []], [[], [], [], []], [[], [], [], []]

    def share(p, ref):
        vcore[p].append(send(ref, ref, other))

    for q in (far2, own2):
        a, b = vrecv[2 * q], vrecv[2 * q + 1]
        merged = jnp.concatenate([a[:, :W - 64], a[:, W - 64:] + b[:, :128], b[:, 128:]], axis=1)
        vall[y, myrows, pl.ds(pl.multiple_of(q * W2, 128), W2)] = merged
    for p in range(4):
        piece = vall.at[y, myrows, pieces[p]]
        ups[p].append(send(piece, piece, device(y=up)))
        downs[p].append(send(piece, piece, device(y=down)))
    for p in range(4):
        share(p, vall.at[y, myrows, pieces[p]])

    unpick_at = lax.broadcasted_iota(jnp.int32, (PW, NVIR), 0)
    for m in range(BINS):
        unpick[pl.ds(m * PW, PW), :] = jnp.where(unpick_at + m * PW == opad, 1.0, 0.0).astype(BF16)

    def relay(step, p):
        from_down, from_up = (y + 8 - step) % 8, (y + step) % 8
        a, b = vall.at[from_down, myrows, pieces[p]], vall.at[from_up, myrows, pieces[p]]
        ups[p][-1].wait_recv()
        if step == 4:
            downs[p][-1].wait_recv()
            share(p, a)
            return
        if step < 3:
            ups[p].append(send(a, a, device(y=up)))
        else:
            half = vall.at[from_down, pl.ds(pl.multiple_of(k * H, 16), H // 2), pieces[p]]
            ups[p].append(send(half, half, device(y=up)))
        downs[p][-1].wait_recv()
        if step < 3:
            downs[p].append(send(b, b, device(y=down)))
        else:
            half = vall.at[from_up, pl.ds(pl.multiple_of(k * H + H // 2, 16), H // 2), pieces[p]]
            downs[p].append(send(half, half, device(y=down)))
        share(p, a)
        share(p, b)

    regroup(0)
    regroup(1)
    for step in range(1, 4):
        for p in range(4):
            relay(step, p)
        regroup(step + 1)
    relay(4, 0)
    relay(4, 1)
    for copies in tcopies:
        for copy in copies:
            copy.wait_recv()

    into = pl.ds(pl.multiple_of(x * PW, 128), PW)

    def multiply(rows, lanes):
        block = vall[:, :, lanes].reshape(8 * W, lanes.size)
        return jnp.dot(trecv[rows, :], block, preferred_element_type=F32).astype(BF16)

    def arrived(*which):
        for p in which:
            for copy in vcore[p]:
                copy.wait_recv()

    arrived(0, 1)
    osend[0] = multiply(pl.ds(0, ROWS), pl.ds(pl.multiple_of(far_lane, 128), W2))
    ocopies = [
        send(osend.at[0, :, pl.ds(same, PW)], orecv.at[:, into], device(x=2 * far2 + x % 2)),
        send(osend.at[0, :, pl.ds(swap, PW)], orecv.at[:, into], device(x=2 * far2 + 1 - x % 2)),
    ]
    relay(4, 2)
    relay(4, 3)
    arrived(2)
    halves = []
    for h in range(2):
        rows = pl.ds(h * 128, 128)
        osend[1, rows, pl.ds(0, PW)] = multiply(rows, pieces[2])
        halves.append(send(osend.at[1, rows, pl.ds(0, PW)], orecv.at[rows, into], device(x=near)))
    arrived(3)
    orecv[:, into] = multiply(pl.ds(0, ROWS), pl.ds(pl.multiple_of(own_lane + same, 128), PW))
    for copy in ocopies:
        copy.wait_recv()
    last, locals_ = [], []
    for h in range(2):
        rows = pl.ds(h * 128, 128)
        halves[h].wait_recv()
        ofull[rows, :] = jnp.dot(orecv[rows, :], unpick[...], preferred_element_type=F32).astype(BF16)
        to = pl.ds(tmine + h * 128, 128)
        last.append(send(ofull.at[rows, pl.ds(theirs, HALF)], out_ref.at[to, :], other))
        local = pltpu.make_async_copy(ofull.at[rows, pl.ds(mine, HALF)], out_ref.at[to, :], local_sem.at[2 + h])
        local.start()
        locals_.append(local)
    for copy in last:
        copy.wait_recv()
    for copy in locals_:
        copy.wait()
    for copy in sent:
        copy.wait_send()


def narrow(
    R, t_ref, v_ref, irreps_ref, out_ref,
    traw, tsend, tmeet, tall, vraw, vpack, vsend, vall, vblock, osend, orecv, ofull,
    pick, vpick, vrow, unpick,
    send_sem, recv_sem, local_sem,
):
    W, W2, RH = 192, 384, R // 2
    tight = R == 192
    YW = 128 if tight else 256
    split = 48 if tight else 80
    pair, virt = lax.axis_index("pair"), lax.axis_index("virt")
    y, zl = pair // 4, pair % 4
    x, zh, k = virt // 4, (virt // 2) % 2, virt % 2

    def device(x=x, y=y, zh=zh, zl=zl, k=k):
        return (y * 4 + zl, (x * 2 + zh) * 2 + k)

    xs = [(x + j) % 4 for j in (2, 1, 3)]
    zs = [(zl + j) % 4 for j in (1, 2, 3)]
    up, down = (y + 1) % 8, (y + 7) % 8
    peers = (
        [device(k=1 - k), device(zh=1 - zh)]
        + [device(x=o) for o in xs] + [device(zl=o) for o in zs] + [device(y=up), device(y=down)]
    )
    barrier = pltpu.get_barrier_semaphore()
    for peer in peers:
        pl.semaphore_signal(barrier, inc=1, device_id=peer, device_id_type=MESH)

    mine = pl.multiple_of(k * HALF, HALF)
    theirs = pl.multiple_of((1 - k) * HALF, HALF)
    vmine, vtheirs = pl.multiple_of(k * 96, 32), pl.multiple_of((1 - k) * 96, 32)
    tmine, ttheirs = pl.multiple_of(k * ROWS, ROWS), pl.multiple_of((1 - k) * ROWS, ROWS)
    other = device(k=1 - k)

    vown = pltpu.make_async_copy(v_ref.at[pl.ds(vmine, 96), :], vraw.at[:, pl.ds(mine, HALF)], local_sem.at[0])
    vown.start()
    town = pltpu.make_async_copy(t_ref.at[pl.ds(tmine, ROWS), :], traw.at[:, pl.ds(mine, HALF)], local_sem.at[1])
    town.start()

    irrep, bins, places = places_of_tiles(irreps_ref)
    padded = [bins[i] * 256 + places[i] for i in range(TILES)]
    again = [jnp.where(places[i] == 128, padded[i] + 64, padded[i]) for i in range(TILES)]

    diff = lax.broadcasted_iota(jnp.int32, (TILE, 1024), 1) - lax.broadcasted_iota(jnp.int32, (TILE, 1024), 0)
    lane = lax.broadcasted_iota(jnp.int32, (1, 1024), 1)
    lane_irrep = jnp.full((1, 1024), -1, jnp.int32)
    for i in range(TILES):
        hit = diff == padded[i] if tight else (diff == padded[i]) | (diff == again[i])
        vpick[pl.ds(i * TILE, TILE), :] = jnp.where(hit, 1.0, 0.0).astype(BF16)
        end = (padded[i] if tight else again[i]) + TILE
        lane_irrep = jnp.where((lane >= padded[i]) & (lane < end), irrep[i], lane_irrep)

    pl.semaphore_wait(barrier, len(peers))

    used = [0]
    sent = []

    def send(src, dst, to):
        n = used[0]
        used[0] += 1
        copy = pltpu.make_async_remote_copy(
            src_ref=src, dst_ref=dst, send_sem=send_sem.at[n], recv_sem=recv_sem.at[n],
            device_id=to, device_id_type=MESH,
        )
        copy.start()
        sent.append(copy)
        return copy

    vraw_copy = send(v_ref.at[pl.ds(vtheirs, 96), :], vraw.at[:, pl.ds(mine, HALF)], other)
    traw_copy = send(t_ref.at[pl.ds(ttheirs, ROWS), :], traw.at[:, pl.ds(mine, HALF)], other)

    vown.wait()
    vraw_copy.wait_recv()
    packed = jnp.dot(vraw[...], vpick[...], preferred_element_type=F32)
    for j in range(3):
        row_irrep = irreps_ref[TILE * (3 * zl + (k * 3 + j) // 2)]
        part = jnp.where(lane_irrep == row_irrep, packed[j * 32:(j + 1) * 32, :], 0.0)
        part = sum(part[:, g * YW:(g + 1) * YW] for g in range(1024 // YW))
        vpack[zl, k, pl.ds(j * 32, 32), :] = part.astype(BF16)
    mypack = vpack.at[zl, k]
    zcopies = [send(mypack, mypack, device(zl=o)) for o in zs]
    dcopies = [send(mypack, mypack, other)]

    for i in range(TILES):
        pick[pl.ds(i * TILE, TILE), :] = jnp.where(diff == padded[i] + (x % 2) * TILE, 1.0, 0.0).astype(BF16)
    into = pl.ds(pl.multiple_of(x * 256, 256), 256)
    tcopies, swaps = [], []

    def scatter(j):
        rows = pl.ds(*PARTS[j])
        tsend[rows, :] = jnp.dot(traw[rows, :], pick[...], preferred_element_type=F32).astype(BF16)
        tcopies.append([
            send(tsend.at[rows, pl.ds(pl.multiple_of(o * 256, 256), 256)], tmeet.at[rows, into], device(x=o)) for o in xs
        ])
        tmeet[rows, into] = tsend[rows, into]

    def swap(j):
        rows = pl.ds(*PARTS[j])
        for copy in tcopies[j]:
            copy.wait_recv()
        for q in range(2):
            a, b = tmeet[rows, pl.ds(512 * q, 256)], tmeet[rows, pl.ds(512 * q + 256, 256)]
            merged = jnp.concatenate([a[:, :128], a[:, 128:] + b[:, :128], b[:, 128:]], axis=1)
            tall[rows, pl.ds(pl.multiple_of(zh * NVIR + q * W2, 128), W2)] = merged
        half = tall.at[rows, pl.ds(pl.multiple_of(zh * NVIR, 128), NVIR)]
        swaps.append(send(half, half, device(zh=1 - zh)))

    town.wait()
    traw_copy.wait_recv()
    scatter(0)
    scatter(1)

    olane = lax.broadcasted_iota(jnp.int32, (1, NVIR), 1)
    oslot = jnp.zeros((1, NVIR), jnp.int32)
    opad = jnp.zeros((1, NVIR), jnp.int32)
    for i in range(TILES):
        here = (olane >= i * TILE) & (olane < (i + 1) * TILE)
        oslot = jnp.where(here, bins[i] * W + places[i] + olane - i * TILE, oslot)
        opad = jnp.where(here, padded[i] + olane - i * TILE, opad)
    r = lax.broadcasted_iota(jnp.int32, (RH, NVIR), 0)
    if tight:
        wants = [k * RH + r]
    else:
        wants = [jnp.where(k == 0, r, jnp.where(r < 48, 144 + r, r - 48)), 48 + r]
    for f, want in enumerate(wants):
        for m in range(BINS):
            vrow[f, pl.ds(m * RH, RH), :] = jnp.where(want + m * W == oslot, 1.0, 0.0).astype(BF16)

    for j, o in enumerate(zs):
        source = (zl + 4 - (1, 2, 3)[j]) % 4
        zcopies[j].wait_recv()
        dcopies.append(send(vpack.at[source, k], vpack.at[source, k], other))

    for copy in dcopies:
        copy.wait_recv()
    full = jnp.concatenate([vpack[z, c] for z in range(4) for c in range(2)], axis=0)
    rows_a = jnp.dot(vrow[0], full, preferred_element_type=F32)
    if tight:
        folded = rows_a
    else:
        rows_b = jnp.dot(vrow[1], full[:, 128:], preferred_element_type=F32)
        at = lax.broadcasted_iota(jnp.int32, (BINS, RH, 128), 1).reshape(BINS * RH, 128)
        low = lax.broadcasted_iota(jnp.int32, (BINS * RH, 128), 1) < 64
        second = (at >= 48 + 144 * (1 - k))
        folded = jnp.where(second, jnp.where(low, rows_a[:, 128:], rows_b), rows_a[:, :128])
    vsend[...] = folded.astype(BF16).reshape(BINS, RH, 128)

    first_row = pl.multiple_of(k * RH, 16)
    myrows = pl.ds(first_row, RH)
    order = [x, xs[0], xs[1], xs[2]]

    def spot(c):
        return (c % 2) * 4 + c // 2

    lanes_of = [pl.ds(pl.multiple_of(a * 128, 128), 128) for a in order]
    xcopies = [send(vsend.at[o], vall.at[spot(y), myrows, lanes_of[0]], device(x=o)) for o in xs]
    vall[spot(y), myrows, lanes_of[0]] = vsend[x]
    vcore, ups, downs = [[], [], [], []], [[], [], [], []], [[], [], [], []]

    def share(p, ref):
        vcore[p].append(send(ref, ref, other))

    def begin(p):
        piece = vall.at[spot(y), myrows, lanes_of[p]]
        ups[p].append(send(piece, piece, device(y=up)))
        downs[p].append(send(piece, piece, device(y=down)))
        share(p, piece)

    def relay(step, p):
        from_down, from_up = spot((y + 8 - step) % 8), spot((y + step) % 8)
        a, b = vall.at[from_down, myrows, lanes_of[p]], vall.at[from_up, myrows, lanes_of[p]]
        ups[p][-1].wait_recv()
        if step == 4:
            downs[p][-1].wait_recv()
            share(p, a)
            return
        if step < 3:
            ups[p].append(send(a, a, device(y=up)))
        else:
            half = vall.at[from_down, pl.ds(first_row, split), lanes_of[p]]
            ups[p].append(send(half, half, device(y=up)))
        downs[p][-1].wait_recv()
        if step < 3:
            downs[p].append(send(b, b, device(y=down)))
        else:
            half = vall.at[from_up, pl.ds(first_row + split, RH - split), lanes_of[p]]
            downs[p].append(send(half, half, device(y=down)))
        share(p, a)
        share(p, b)

    begin(0)
    swap(0)
    scatter(2)
    arrivals = {1: 0, 2: 2, 3: 1}
    for p in (2, 3, 1):
        xcopies[arrivals[p]].wait_recv()
        begin(p)
    swap(1)
    scatter(3)

    unpick_at = lax.broadcasted_iota(jnp.int32, (256, NVIR), 0)
    for m in range(BINS):
        unpick[pl.ds(m * 256, 256), :] = jnp.where(unpick_at + m * 256 == opad, 1.0, 0.0).astype(BF16)

    def expand(p):
        for copy in vcore[p]:
            copy.wait_recv()
        v = vall[:, :, lanes_of[p]]
        if tight:
            left = jnp.concatenate([v[:, :128], jnp.zeros((8, 64, 128), BF16)], axis=1)
            right = jnp.concatenate([jnp.zeros((8, 128, 128), BF16), v[:, 128:]], axis=1)
        else:
            left, fold = v[:, :192], v[:, 192:]
            turned = pltpu.roll(fold.astype(F32).reshape(8 * 96, 128), 64, 1).astype(BF16).reshape(8, 96, 128)
            right = jnp.concatenate([fold, turned], axis=1)
        vblock[p, :, 0:128] = left.reshape(8 * W, 128)
        vblock[p, :, 128:256] = right.reshape(8 * W, 128)

    ocopies = [[] for _ in BLOCKS]

    def output(p):
        expand(p)
        product = jnp.dot(tall[...], vblock[p], preferred_element_type=F32).astype(BF16)
        if p == 0:
            orecv[:, into] = product
            return
        osend[p - 1] = product
        for b, block in enumerate(BLOCKS):
            rows = pl.ds(*block)
            ocopies[b].append(send(osend.at[p - 1, rows, :], orecv.at[rows, into], device(x=order[p])))

    last, locals_ = [], []

    def finish(b):
        first, count = BLOCKS[b]
        rows, to = pl.ds(first, count), pl.ds(tmine + first, count)
        for copy in ocopies[b]:
            copy.wait_recv()
        ofull[rows, :] = jnp.dot(orecv[rows, :], unpick[...], preferred_element_type=F32).astype(BF16)
        last.append(send(ofull.at[rows, pl.ds(theirs, HALF)], out_ref.at[to, :], other))
        local = pltpu.make_async_copy(ofull.at[rows, pl.ds(mine, HALF)], out_ref.at[to, :], local_sem.at[2 + b])
        local.start()
        locals_.append(local)

    for step in range(1, 4):
        for p in TURN:
            relay(step, p)
        if step < 3:
            swap(step + 1)
    for copy in swaps:
        copy.wait_recv()
    relay(4, TURN[0])
    relay(4, TURN[1])
    output(TURN[0])
    relay(4, TURN[2])
    output(TURN[1])
    relay(4, TURN[3])
    output(TURN[2])
    output(TURN[3])
    finish(0)
    finish(1)
    for copy in last:
        copy.wait_recv()
    for copy in locals_:
        copy.wait()
    for copy in sent:
        copy.wait_send()


PARTS = ((0, 64), (64, 64), (128, 64), (192, 64))
BLOCKS = ((0, 128), (128, 128))
TURN = (2, 3, 1, 0)


def ladder(width, amplitudes, integrals, irreps):
    vmem = lambda *shape: pltpu.VMEM(shape, BF16)
    W, PW, W2, H = width, width + 64, 2 * width, width // 2
    return pl.pallas_call(
        functools.partial(kernel, W),
        out_shape=jax.ShapeDtypeStruct((512, HALF), BF16),
        in_specs=[
            pl.BlockSpec(memory_space=pl.ANY), pl.BlockSpec(memory_space=pl.ANY),
            pl.BlockSpec(memory_space=pltpu.SMEM),
        ],
        out_specs=pl.BlockSpec(memory_space=pl.ANY),
        scratch_shapes=[
            vmem(2, ROWS, NVIR), vmem(ROWS, 4 * W2), vmem(ROWS, 4 * W2), vmem(ROWS, 4 * W2),
            vmem(96, NVIR), vmem(4, 2, 96, PW), vmem(BINS, H, PW), vmem(4, H, PW), vmem(8, W, 4 * W),
            vmem(2, ROWS, W2), vmem(ROWS, 4 * PW), vmem(ROWS, NVIR),
            vmem(2, NVIR, 4 * W2), vmem(NVIR, 4 * PW), vmem(4 * H, NVIR), vmem(4 * PW, NVIR),
            pltpu.SemaphoreType.DMA((SEMS,)), pltpu.SemaphoreType.DMA((SEMS,)), pltpu.SemaphoreType.DMA((4,)),
        ],
        compiler_params=pltpu.CompilerParams(
            collective_id=width // 300, has_side_effects=True, vmem_limit_bytes=56 << 20
        ),
        name="ladder%d" % width,
    )(amplitudes, integrals, irreps)


def narrow_ladder(packed_rows, amplitudes, integrals, irreps):
    vmem = lambda *shape: pltpu.VMEM(shape, BF16)
    tight = packed_rows == 192
    half = packed_rows // 2
    return pl.pallas_call(
        functools.partial(narrow, packed_rows),
        out_shape=jax.ShapeDtypeStruct((512, HALF), BF16),
        in_specs=[
            pl.BlockSpec(memory_space=pl.ANY), pl.BlockSpec(memory_space=pl.ANY),
            pl.BlockSpec(memory_space=pltpu.SMEM),
        ],
        out_specs=pl.BlockSpec(memory_space=pl.ANY),
        scratch_shapes=[
            vmem(ROWS, NVIR), vmem(ROWS, 1024), vmem(ROWS, 1024), vmem(ROWS, 1536),
            vmem(96, NVIR), vmem(4, 2, 96, 128 if tight else 256), vmem(BINS, half, 128), vmem(8, packed_rows, 512),
            vmem(4, 1536, 256), vmem(3, ROWS, 256), vmem(ROWS, 1024), vmem(ROWS, NVIR),
            vmem(NVIR, 1024), vmem(NVIR, 1024), vmem(1 if tight else 2, 4 * half, NVIR), vmem(1024, NVIR),
            pltpu.SemaphoreType.DMA((SEMS,)), pltpu.SemaphoreType.DMA((SEMS,)), pltpu.SemaphoreType.DMA((4,)),
        ],
        compiler_params=pltpu.CompilerParams(
            collective_id=2 if tight else 3, has_side_effects=True, vmem_limit_bytes=56 << 20
        ),
        name="narrow%d" % packed_rows,
    )(amplitudes, integrals, irreps)


def per_device(amplitudes, integrals, irreps):
    ahead = jnp.pad(irreps, (0, 64), constant_values=-1)
    over = (irreps[:-128] == irreps[128:]).astype(jnp.int32) + (irreps[:-128] == ahead[192:]).astype(jnp.int32)
    kernels = [functools.partial(narrow_ladder, 192), functools.partial(narrow_ladder, 288), functools.partial(ladder, 320)]
    return lax.switch(jnp.max(over), kernels, amplitudes, integrals, irreps)


def solution(mesh):
    placed = (P("pair", "virt"), P("pair", "virt"), P())
    return jax.shard_map(
        per_device, mesh=mesh, in_specs=placed, out_specs=P("pair", "virt"), check_vma=False
    )
```

```python
import functools

import jax
import jax.numpy as jnp
from jax import lax
from jax.experimental import pallas as pl
from jax.experimental.pallas import tpu as pltpu
from jax.sharding import PartitionSpec as P

MESH = pl.DeviceIdType.MESH
BF16 = jnp.bfloat16
F32 = jnp.float32
TILE = 64
TILES = 12
BINS = 4
NVIR = 768
HALF = 384
ROWS = 256
CHUNKS = ((0, 32), (32, 32), (64, 64), (128, 64), (192, 64))
SEMS = 128


def places_of_tiles(irreps_ref):
    irrep = [irreps_ref[TILE * i] for i in range(TILES)]
    count = [sum((irrep[i] == g).astype(jnp.int32) for i in range(TILES)) for g in range(8)]
    big = [(c >= 3).astype(jnp.int32) for c in count]
    two = [(c == 2).astype(jnp.int32) for c in count]
    one = [(c == 1).astype(jnp.int32) for c in count]
    n3, n2 = sum(big), sum(two)
    bins, places = [jnp.int32(0)] * TILES, [jnp.int32(0)] * TILES
    start = r3 = r2 = r1 = jnp.int32(0)
    for g in range(8):
        lone = jnp.where(r1 < n2, 3 * (n3 + r1) + 2, 3 * (n3 + n2) + r1 - n2)
        base = jnp.where(big[g] == 1, 3 * r3, jnp.where(two[g] == 1, 3 * (n3 + r2), lone))
        for i in range(TILES):
            here = irrep[i] == g
            bins[i] = jnp.where(here, base // 3, bins[i])
            places[i] = jnp.where(here, (base % 3 + i - start) * TILE, places[i])
        start, r3, r2, r1 = start + count[g], r3 + big[g], r2 + two[g], r1 + one[g]
    return irrep, bins, places


def kernel(
    W, t_ref, v_ref, irreps_ref, out_ref,
    traw, tpart, tsend, trecv, vraw, vpack, vsend, vrecv, vall, osend, orecv, ofull,
    pick, vpick, vrow, unpick,
    send_sem, recv_sem, local_sem,
):
    PW, W2, H = W + 64, 2 * W, W // 2
    pair, virt = lax.axis_index("pair"), lax.axis_index("virt")
    y, zl = pair // 4, pair % 4
    x, zh, k = virt // 4, (virt // 2) % 2, virt % 2

    def device(x=x, y=y, zh=zh, zl=zl, k=k):
        return (y * 4 + zl, (x * 2 + zh) * 2 + k)

    near = x + 1 - 2 * (x % 2)
    own2, far2 = x // 2, 1 - x // 2
    xs = [(x + j) % 4 for j in (2, 1, 3)]
    zs = [(zl + j) % 4 for j in (1, 2, 3)]
    up, down = (y + 1) % 8, (y + 7) % 8
    peers = (
        [device(k=1 - k), device(zh=1 - zh), device(zh=1 - zh, k=1 - k)]
        + [device(x=o) for o in xs] + [device(zl=o) for o in zs] + [device(y=up), device(y=down)]
    )
    barrier = pltpu.get_barrier_semaphore()
    for peer in peers:
        pl.semaphore_signal(barrier, inc=1, device_id=peer, device_id_type=MESH)

    mine = pl.multiple_of(k * HALF, HALF)
    theirs = pl.multiple_of((1 - k) * HALF, HALF)
    vmine, vtheirs = pl.multiple_of(k * 96, 32), pl.multiple_of((1 - k) * 96, 32)
    tmine, ttheirs = pl.multiple_of(k * ROWS, ROWS), pl.multiple_of((1 - k) * ROWS, ROWS)
    other = device(k=1 - k)

    vown = pltpu.make_async_copy(v_ref.at[pl.ds(vmine, 96), :], vraw.at[:, pl.ds(mine, HALF)], local_sem.at[0])
    vown.start()
    town = pltpu.make_async_copy(t_ref.at[pl.ds(tmine, ROWS), :], traw.at[0, :, pl.ds(mine, HALF)], local_sem.at[1])
    town.start()

    irrep, bins, places = places_of_tiles(irreps_ref)
    shift = (x % 2) * TILE
    padded = [bins[i] * PW + shift + places[i] for i in range(TILES)]

    diff = lax.broadcasted_iota(jnp.int32, (TILE, 4 * PW), 1) - lax.broadcasted_iota(jnp.int32, (TILE, 4 * PW), 0)
    for i in range(TILES):
        vpick[pl.ds(i * TILE, TILE), :] = jnp.where(diff == padded[i], 1.0, 0.0).astype(BF16)
    lane = lax.broadcasted_iota(jnp.int32, (1, 4 * PW), 1)
    lane_irrep = jnp.full((1, 4 * PW), -1, jnp.int32)
    for i in range(TILES):
        lane_irrep = jnp.where((lane >= padded[i]) & (lane < padded[i] + TILE), irrep[i], lane_irrep)

    pl.semaphore_wait(barrier, len(peers))

    used = [0]
    sent = []

    def send(src, dst, to):
        n = used[0]
        used[0] += 1
        copy = pltpu.make_async_remote_copy(
            src_ref=src, dst_ref=dst, send_sem=send_sem.at[n], recv_sem=recv_sem.at[n],
            device_id=to, device_id_type=MESH,
        )
        copy.start()
        sent.append(copy)
        return copy

    far_copies = []

    def send_far(j):
        first, count = CHUNKS[j]
        dst = traw.at[1, pl.ds(first, count), pl.ds(mine, HALF)]
        far_copies.append([
            send(t_ref.at[pl.ds(tmine + first, count), :], dst, device(zh=1 - zh)),
            send(t_ref.at[pl.ds(ttheirs + first, count), :], dst, device(zh=1 - zh, k=1 - k)),
        ])

    vraw_copy = send(v_ref.at[pl.ds(vtheirs, 96), :], vraw.at[:, pl.ds(mine, HALF)], other)
    traw_copy = send(t_ref.at[pl.ds(ttheirs, ROWS), :], traw.at[0, :, pl.ds(mine, HALF)], other)

    vown.wait()
    vraw_copy.wait_recv()
    packed = jnp.dot(vraw[...], vpick[...], preferred_element_type=F32)
    for j in range(3):
        row_irrep = irreps_ref[TILE * (3 * zl + (k * 3 + j) // 2)]
        part = jnp.where(lane_irrep == row_irrep, packed[j * 32:(j + 1) * 32, :], 0.0)
        part = part[:, 0:PW] + part[:, PW:2 * PW] + part[:, 2 * PW:3 * PW] + part[:, 3 * PW:4 * PW]
        vpack[zl, k, pl.ds(j * 32, 32), :] = part.astype(BF16)
    mypack = vpack.at[zl, k]
    zcopies = [send(mypack, mypack, device(zl=o)) for o in zs]
    dcopies = [send(mypack, mypack, other)]

    olane = lax.broadcasted_iota(jnp.int32, (1, NVIR), 1)
    oslot = jnp.zeros((1, NVIR), jnp.int32)
    opad = jnp.zeros((1, NVIR), jnp.int32)
    for i in range(TILES):
        here = (olane >= i * TILE) & (olane < (i + 1) * TILE)
        oslot = jnp.where(here, bins[i] * W + places[i] + olane - i * TILE, oslot)
        opad = jnp.where(here, padded[i] + olane - i * TILE, opad)
    for m in range(BINS):
        want = lax.broadcasted_iota(jnp.int32, (H, NVIR), 0) + m * W + k * H
        vrow[pl.ds(m * H, H), :] = jnp.where(want == oslot, 1.0, 0.0).astype(BF16)

    wide = lax.broadcasted_iota(jnp.int32, (TILE, 4 * W2), 1) - lax.broadcasted_iota(jnp.int32, (TILE, 4 * W2), 0)
    for h in range(2):
        offset = (zh if h == 0 else 1 - zh) * W
        for i in range(TILES):
            pick[h, pl.ds(i * TILE, TILE), :] = jnp.where(wide == bins[i] * W2 + offset + places[i], 1.0, 0.0).astype(BF16)

    for j, o in enumerate(zs):
        source = (zl + 4 - (1, 2, 3)[j]) % 4
        zcopies[j].wait_recv()
        dcopies.append(send(vpack.at[source, k], vpack.at[source, k], other))
    for j in range(len(CHUNKS)):
        send_far(j)

    town.wait()
    traw_copy.wait_recv()
    tpart[...] = jnp.dot(traw[0], pick[0], preferred_element_type=F32).astype(BF16)

    for copy in dcopies:
        copy.wait_recv()
    full = jnp.concatenate([vpack[z, c] for z in range(4) for c in range(2)], axis=0)
    vsend[...] = jnp.dot(vrow[...], full, preferred_element_type=F32).astype(BF16).reshape(BINS, H, PW)
    xcopies = [send(vsend.at[o], vrecv.at[x], device(x=o)) for o in xs]
    vrecv[x] = vsend[x]

    tcopies = []

    def regroup(j):
        rows = pl.ds(*CHUNKS[j])
        for copy in far_copies[j]:
            copy.wait_recv()
        tsend[rows, :] = tpart[rows, :] + jnp.dot(traw[1, rows, :], pick[1], preferred_element_type=F32).astype(BF16)
        own = pl.ds(pl.multiple_of(x * W2, W2), W2)
        tcopies.append([
            send(tsend.at[rows, pl.ds(pl.multiple_of(o * W2, W2), W2)], trecv.at[rows, own], device(x=o)) for o in xs
        ])
        trecv[rows, own] = tsend[rows, own]

    for copy in xcopies:
        copy.wait_recv()
    myrows = pl.ds(pl.multiple_of(k * H, 16), H)
    same = pl.multiple_of((x % 2) * (W2 - PW), 128)
    swap = pl.multiple_of((1 - x % 2) * (W2 - PW), 128)
    far_lane, own_lane = far2 * W2, own2 * W2
    pieces = [
        pl.ds(pl.multiple_of(far_lane, 128), PW),
        pl.ds(pl.multiple_of(far_lane + PW, 128), W2 - PW),
        pl.ds(pl.multiple_of(own_lane + swap, 128), PW),
        pl.ds(pl.multiple_of(own_lane + (x % 2) * PW, 128), W2 - PW),
    ]
    vcore, ups, downs = [[], [], [], []], [[], [], [], []], [[], [], [], []]

    def share(p, ref):
        vcore[p].append(send(ref, ref, other))

    for q in (far2, own2):
        a, b = vrecv[2 * q], vrecv[2 * q + 1]
        merged = jnp.concatenate([a[:, :W - 64], a[:, W - 64:] + b[:, :128], b[:, 128:]], axis=1)
        vall[y, myrows, pl.ds(pl.multiple_of(q * W2, 128), W2)] = merged
    for p in range(4):
        piece = vall.at[y, myrows, pieces[p]]
        ups[p].append(send(piece, piece, device(y=up)))
        downs[p].append(send(piece, piece, device(y=down)))
    for p in range(4):
        share(p, vall.at[y, myrows, pieces[p]])

    unpick_at = lax.broadcasted_iota(jnp.int32, (PW, NVIR), 0)
    for m in range(BINS):
        unpick[pl.ds(m * PW, PW), :] = jnp.where(unpick_at + m * PW == opad, 1.0, 0.0).astype(BF16)

    def relay(step, p):
        from_down, from_up = (y + 8 - step) % 8, (y + step) % 8
        a, b = vall.at[from_down, myrows, pieces[p]], vall.at[from_up, myrows, pieces[p]]
        ups[p][-1].wait_recv()
        if step == 4:
            downs[p][-1].wait_recv()
            share(p, a)
            return
        if step < 3:
            ups[p].append(send(a, a, device(y=up)))
        else:
            half = vall.at[from_down, pl.ds(pl.multiple_of(k * H, 16), H // 2), pieces[p]]
            ups[p].append(send(half, half, device(y=up)))
        downs[p][-1].wait_recv()
        if step < 3:
            downs[p].append(send(b, b, device(y=down)))
        else:
            half = vall.at[from_up, pl.ds(pl.multiple_of(k * H + H // 2, 16), H // 2), pieces[p]]
            downs[p].append(send(half, half, device(y=down)))
        share(p, a)
        share(p, b)

    regroup(0)
    regroup(1)
    for step in range(1, 4):
        for p in range(4):
            relay(step, p)
        regroup(step + 1)
    relay(4, 0)
    relay(4, 1)
    for copies in tcopies:
        for copy in copies:
            copy.wait_recv()

    into = pl.ds(pl.multiple_of(x * PW, 128), PW)

    def multiply(rows, lanes):
        block = vall[:, :, lanes].reshape(8 * W, lanes.size)
        return jnp.dot(trecv[rows, :], block, preferred_element_type=F32).astype(BF16)

    def arrived(*which):
        for p in which:
            for copy in vcore[p]:
                copy.wait_recv()

    arrived(0, 1)
    osend[0] = multiply(pl.ds(0, ROWS), pl.ds(pl.multiple_of(far_lane, 128), W2))
    ocopies = [
        send(osend.at[0, :, pl.ds(same, PW)], orecv.at[:, into], device(x=2 * far2 + x % 2)),
        send(osend.at[0, :, pl.ds(swap, PW)], orecv.at[:, into], device(x=2 * far2 + 1 - x % 2)),
    ]
    relay(4, 2)
    relay(4, 3)
    arrived(2)
    halves = []
    for h in range(2):
        rows = pl.ds(h * 128, 128)
        osend[1, rows, pl.ds(0, PW)] = multiply(rows, pieces[2])
        halves.append(send(osend.at[1, rows, pl.ds(0, PW)], orecv.at[rows, into], device(x=near)))
    arrived(3)
    orecv[:, into] = multiply(pl.ds(0, ROWS), pl.ds(pl.multiple_of(own_lane + same, 128), PW))
    for copy in ocopies:
        copy.wait_recv()
    last, locals_ = [], []
    for h in range(2):
        rows = pl.ds(h * 128, 128)
        halves[h].wait_recv()
        ofull[rows, :] = jnp.dot(orecv[rows, :], unpick[...], preferred_element_type=F32).astype(BF16)
        to = pl.ds(tmine + h * 128, 128)
        last.append(send(ofull.at[rows, pl.ds(theirs, HALF)], out_ref.at[to, :], other))
        local = pltpu.make_async_copy(ofull.at[rows, pl.ds(mine, HALF)], out_ref.at[to, :], local_sem.at[2 + h])
        local.start()
        locals_.append(local)
    for copy in last:
        copy.wait_recv()
    for copy in locals_:
        copy.wait()
    for copy in sent:
        copy.wait_send()


def narrow(
    R, t_ref, v_ref, irreps_ref, out_ref,
    traw, tsend, tmeet, tall, vraw, vpack, vsend, vall, vblock, osend, orecv, ofull,
    pick, vpick, vrow, unpick,
    send_sem, recv_sem, local_sem,
):
    W, W2, RH = 192, 384, R // 2
    tight = R == 192
    YW = 128 if tight else 256
    split = 48 if tight else 80
    pair, virt = lax.axis_index("pair"), lax.axis_index("virt")
    y, zl = pair // 4, pair % 4
    x, zh, k = virt // 4, (virt // 2) % 2, virt % 2

    def device(x=x, y=y, zh=zh, zl=zl, k=k):
        return (y * 4 + zl, (x * 2 + zh) * 2 + k)

    xs = [(x + j) % 4 for j in (2, 1, 3)]
    zs = [(zl + j) % 4 for j in (1, 2, 3)]
    up, down = (y + 1) % 8, (y + 7) % 8
    peers = (
        [device(k=1 - k), device(zh=1 - zh)]
        + [device(x=o) for o in xs] + [device(zl=o) for o in zs] + [device(y=up), device(y=down)]
    )
    barrier = pltpu.get_barrier_semaphore()
    for peer in peers:
        pl.semaphore_signal(barrier, inc=1, device_id=peer, device_id_type=MESH)

    mine = pl.multiple_of(k * HALF, HALF)
    theirs = pl.multiple_of((1 - k) * HALF, HALF)
    vmine, vtheirs = pl.multiple_of(k * 96, 32), pl.multiple_of((1 - k) * 96, 32)
    tmine, ttheirs = pl.multiple_of(k * ROWS, ROWS), pl.multiple_of((1 - k) * ROWS, ROWS)
    other = device(k=1 - k)

    vown = pltpu.make_async_copy(v_ref.at[pl.ds(vmine, 96), :], vraw.at[:, pl.ds(mine, HALF)], local_sem.at[0])
    vown.start()
    town = pltpu.make_async_copy(t_ref.at[pl.ds(tmine, ROWS), :], traw.at[:, pl.ds(mine, HALF)], local_sem.at[1])
    town.start()

    irrep, bins, places = places_of_tiles(irreps_ref)
    padded = [bins[i] * 256 + places[i] for i in range(TILES)]
    again = [jnp.where(places[i] == 128, padded[i] + 64, padded[i]) for i in range(TILES)]

    diff = lax.broadcasted_iota(jnp.int32, (TILE, 1024), 1) - lax.broadcasted_iota(jnp.int32, (TILE, 1024), 0)
    lane = lax.broadcasted_iota(jnp.int32, (1, 1024), 1)
    lane_irrep = jnp.full((1, 1024), -1, jnp.int32)
    for i in range(TILES):
        hit = diff == padded[i] if tight else (diff == padded[i]) | (diff == again[i])
        vpick[pl.ds(i * TILE, TILE), :] = jnp.where(hit, 1.0, 0.0).astype(BF16)
        end = (padded[i] if tight else again[i]) + TILE
        lane_irrep = jnp.where((lane >= padded[i]) & (lane < end), irrep[i], lane_irrep)

    pl.semaphore_wait(barrier, len(peers))

    used = [0]
    sent = []

    def send(src, dst, to):
        n = used[0]
        used[0] += 1
        copy = pltpu.make_async_remote_copy(
            src_ref=src, dst_ref=dst, send_sem=send_sem.at[n], recv_sem=recv_sem.at[n],
            device_id=to, device_id_type=MESH,
        )
        copy.start()
        sent.append(copy)
        return copy

    vraw_copy = send(v_ref.at[pl.ds(vtheirs, 96), :], vraw.at[:, pl.ds(mine, HALF)], other)
    traw_copy = send(t_ref.at[pl.ds(ttheirs, ROWS), :], traw.at[:, pl.ds(mine, HALF)], other)

    vown.wait()
    vraw_copy.wait_recv()
    packed = jnp.dot(vraw[...], vpick[...], preferred_element_type=F32)
    for j in range(3):
        row_irrep = irreps_ref[TILE * (3 * zl + (k * 3 + j) // 2)]
        part = jnp.where(lane_irrep == row_irrep, packed[j * 32:(j + 1) * 32, :], 0.0)
        part = sum(part[:, g * YW:(g + 1) * YW] for g in range(1024 // YW))
        vpack[zl, k, pl.ds(j * 32, 32), :] = part.astype(BF16)
    mypack = vpack.at[zl, k]
    zcopies = [send(mypack, mypack, device(zl=o)) for o in zs]
    dcopies = [send(mypack, mypack, other)]

    for i in range(TILES):
        pick[pl.ds(i * TILE, TILE), :] = jnp.where(diff == padded[i] + (x % 2) * TILE, 1.0, 0.0).astype(BF16)
    into = pl.ds(pl.multiple_of(x * 256, 256), 256)
    tcopies, swaps = [], []

    def scatter(j):
        rows = pl.ds(*PARTS[j])
        tsend[rows, :] = jnp.dot(traw[rows, :], pick[...], preferred_element_type=F32).astype(BF16)
        tcopies.append([
            send(tsend.at[rows, pl.ds(pl.multiple_of(o * 256, 256), 256)], tmeet.at[rows, into], device(x=o)) for o in xs
        ])
        tmeet[rows, into] = tsend[rows, into]

    def swap(j):
        rows = pl.ds(*PARTS[j])
        for copy in tcopies[j]:
            copy.wait_recv()
        for q in range(2):
            a, b = tmeet[rows, pl.ds(512 * q, 256)], tmeet[rows, pl.ds(512 * q + 256, 256)]
            merged = jnp.concatenate([a[:, :128], a[:, 128:] + b[:, :128], b[:, 128:]], axis=1)
            tall[rows, pl.ds(pl.multiple_of(zh * NVIR + q * W2, 128), W2)] = merged
        half = tall.at[rows, pl.ds(pl.multiple_of(zh * NVIR, 128), NVIR)]
        swaps.append(send(half, half, device(zh=1 - zh)))

    town.wait()
    traw_copy.wait_recv()
    scatter(0)
    scatter(1)

    olane = lax.broadcasted_iota(jnp.int32, (1, NVIR), 1)
    oslot = jnp.zeros((1, NVIR), jnp.int32)
    opad = jnp.zeros((1, NVIR), jnp.int32)
    for i in range(TILES):
        here = (olane >= i * TILE) & (olane < (i + 1) * TILE)
        oslot = jnp.where(here, bins[i] * W + places[i] + olane - i * TILE, oslot)
        opad = jnp.where(here, padded[i] + olane - i * TILE, opad)
    r = lax.broadcasted_iota(jnp.int32, (RH, NVIR), 0)
    if tight:
        wants = [k * RH + r]
    else:
        wants = [jnp.where(k == 0, r, jnp.where(r < 48, 144 + r, r - 48)), 48 + r]
    for f, want in enumerate(wants):
        for m in range(BINS):
            vrow[f, pl.ds(m * RH, RH), :] = jnp.where(want + m * W == oslot, 1.0, 0.0).astype(BF16)

    for j, o in enumerate(zs):
        source = (zl + 4 - (1, 2, 3)[j]) % 4
        zcopies[j].wait_recv()
        dcopies.append(send(vpack.at[source, k], vpack.at[source, k], other))

    for copy in dcopies:
        copy.wait_recv()
    full = jnp.concatenate([vpack[z, c] for z in range(4) for c in range(2)], axis=0)
    rows_a = jnp.dot(vrow[0], full, preferred_element_type=F32)
    if tight:
        folded = rows_a
    else:
        rows_b = jnp.dot(vrow[1], full[:, 128:], preferred_element_type=F32)
        at = lax.broadcasted_iota(jnp.int32, (BINS, RH, 128), 1).reshape(BINS * RH, 128)
        low = lax.broadcasted_iota(jnp.int32, (BINS * RH, 128), 1) < 64
        second = (at >= 48 + 144 * (1 - k))
        folded = jnp.where(second, jnp.where(low, rows_a[:, 128:], rows_b), rows_a[:, :128])
    vsend[...] = folded.astype(BF16).reshape(BINS, RH, 128)

    first_row = pl.multiple_of(k * RH, 16)
    myrows = pl.ds(first_row, RH)
    order = [x, xs[0], xs[1], xs[2]]

    def spot(c):
        return (c % 2) * 4 + c // 2

    lanes_of = [pl.ds(pl.multiple_of(a * 128, 128), 128) for a in order]
    xcopies = [send(vsend.at[o], vall.at[spot(y), myrows, lanes_of[0]], device(x=o)) for o in xs]
    vall[spot(y), myrows, lanes_of[0]] = vsend[x]
    whole, vcore, ups, downs = [], [[], [], [], []], [[], [], [], []], [[], [], [], []]

    def share(c):
        block = vall.at[spot(c), myrows]
        whole.append(send(block, block, other))

    def begin(p):
        piece = vall.at[spot(y), myrows, lanes_of[p]]
        ups[p].append(send(piece, piece, device(y=up)))
        downs[p].append(send(piece, piece, device(y=down)))

    def relay(step, p):
        from_down, from_up = spot((y + 8 - step) % 8), spot((y + step) % 8)
        a, b = vall.at[from_down, myrows, lanes_of[p]], vall.at[from_up, myrows, lanes_of[p]]
        ups[p][-1].wait_recv()
        if step == 4:
            downs[p][-1].wait_recv()
            vcore[p].append(send(a, a, other))
            return
        if step < 3:
            ups[p].append(send(a, a, device(y=up)))
        else:
            half = vall.at[from_down, pl.ds(first_row, split), lanes_of[p]]
            ups[p].append(send(half, half, device(y=up)))
        downs[p][-1].wait_recv()
        if step < 3:
            downs[p].append(send(b, b, device(y=down)))
        else:
            half = vall.at[from_up, pl.ds(first_row + split, RH - split), lanes_of[p]]
            downs[p].append(send(half, half, device(y=down)))

    begin(0)
    swap(0)
    scatter(2)
    arrivals = {1: 0, 2: 2, 3: 1}
    for p in (2, 3, 1):
        xcopies[arrivals[p]].wait_recv()
        begin(p)
    share(y)
    swap(1)
    scatter(3)
    swap(2)

    unpick_at = lax.broadcasted_iota(jnp.int32, (256, NVIR), 0)
    for m in range(BINS):
        unpick[pl.ds(m * 256, 256), :] = jnp.where(unpick_at + m * 256 == opad, 1.0, 0.0).astype(BF16)

    def expand(p):
        while whole:
            whole.pop(0).wait_recv()
        for copy in vcore[p]:
            copy.wait_recv()
        v = vall[:, :, lanes_of[p]]
        if tight:
            left = jnp.concatenate([v[:, :128], jnp.zeros((8, 64, 128), BF16)], axis=1)
            right = jnp.concatenate([jnp.zeros((8, 128, 128), BF16), v[:, 128:]], axis=1)
        else:
            left, fold = v[:, :192], v[:, 192:]
            turned = pltpu.roll(fold.astype(F32).reshape(8 * 96, 128), 64, 1).astype(BF16).reshape(8, 96, 128)
            right = jnp.concatenate([fold, turned], axis=1)
        vblock[p, :, 0:128] = left.reshape(8 * W, 128)
        vblock[p, :, 128:256] = right.reshape(8 * W, 128)

    ocopies = [[] for _ in BLOCKS]

    def output(p):
        expand(p)
        product = jnp.dot(tall[...], vblock[p], preferred_element_type=F32).astype(BF16)
        if p == 0:
            orecv[:, into] = product
            return
        osend[p - 1] = product
        for b, block in enumerate(BLOCKS):
            rows = pl.ds(*block)
            ocopies[b].append(send(osend.at[p - 1, rows, :], orecv.at[rows, into], device(x=order[p])))

    last, locals_ = [], []

    def finish(b):
        first, count = BLOCKS[b]
        rows, to = pl.ds(first, count), pl.ds(tmine + first, count)
        for copy in ocopies[b]:
            copy.wait_recv()
        ofull[rows, :] = jnp.dot(orecv[rows, :], unpick[...], preferred_element_type=F32).astype(BF16)
        last.append(send(ofull.at[rows, pl.ds(theirs, HALF)], out_ref.at[to, :], other))
        local = pltpu.make_async_copy(ofull.at[rows, pl.ds(mine, HALF)], out_ref.at[to, :], local_sem.at[2 + b])
        local.start()
        locals_.append(local)

    for step in range(1, 4):
        for p in TURN:
            relay(step, p)
        share((y + 8 - step) % 8)
        share((y + step) % 8)
        if step == 1:
            swap(3)
    relay(4, TURN[0])
    relay(4, TURN[1])
    for copy in swaps:
        copy.wait_recv()
    output(TURN[0])
    relay(4, TURN[2])
    output(TURN[1])
    relay(4, TURN[3])
    output(TURN[2])
    output(TURN[3])
    finish(0)
    finish(1)
    for copy in last:
        copy.wait_recv()
    for copy in locals_:
        copy.wait()
    for copy in sent:
        copy.wait_send()


PARTS = ((0, 64), (64, 64), (128, 64), (192, 64))
BLOCKS = ((0, 128), (128, 128))
TURN = (2, 3, 1, 0)


def ladder(width, amplitudes, integrals, irreps):
    vmem = lambda *shape: pltpu.VMEM(shape, BF16)
    W, PW, W2, H = width, width + 64, 2 * width, width // 2
    return pl.pallas_call(
        functools.partial(kernel, W),
        out_shape=jax.ShapeDtypeStruct((512, HALF), BF16),
        in_specs=[
            pl.BlockSpec(memory_space=pl.ANY), pl.BlockSpec(memory_space=pl.ANY),
            pl.BlockSpec(memory_space=pltpu.SMEM),
        ],
        out_specs=pl.BlockSpec(memory_space=pl.ANY),
        scratch_shapes=[
            vmem(2, ROWS, NVIR), vmem(ROWS, 4 * W2), vmem(ROWS, 4 * W2), vmem(ROWS, 4 * W2),
            vmem(96, NVIR), vmem(4, 2, 96, PW), vmem(BINS, H, PW), vmem(4, H, PW), vmem(8, W, 4 * W),
            vmem(2, ROWS, W2), vmem(ROWS, 4 * PW), vmem(ROWS, NVIR),
            vmem(2, NVIR, 4 * W2), vmem(NVIR, 4 * PW), vmem(4 * H, NVIR), vmem(4 * PW, NVIR),
            pltpu.SemaphoreType.DMA((SEMS,)), pltpu.SemaphoreType.DMA((SEMS,)), pltpu.SemaphoreType.DMA((4,)),
        ],
        compiler_params=pltpu.CompilerParams(
            collective_id=width // 300, has_side_effects=True, vmem_limit_bytes=56 << 20
        ),
        name="ladder%d" % width,
    )(amplitudes, integrals, irreps)


def narrow_ladder(packed_rows, amplitudes, integrals, irreps):
    vmem = lambda *shape: pltpu.VMEM(shape, BF16)
    tight = packed_rows == 192
    half = packed_rows // 2
    return pl.pallas_call(
        functools.partial(narrow, packed_rows),
        out_shape=jax.ShapeDtypeStruct((512, HALF), BF16),
        in_specs=[
            pl.BlockSpec(memory_space=pl.ANY), pl.BlockSpec(memory_space=pl.ANY),
            pl.BlockSpec(memory_space=pltpu.SMEM),
        ],
        out_specs=pl.BlockSpec(memory_space=pl.ANY),
        scratch_shapes=[
            vmem(ROWS, NVIR), vmem(ROWS, 1024), vmem(ROWS, 1024), vmem(ROWS, 1536),
            vmem(96, NVIR), vmem(4, 2, 96, 128 if tight else 256), vmem(BINS, half, 128), vmem(8, packed_rows, 512),
            vmem(4, 1536, 256), vmem(3, ROWS, 256), vmem(ROWS, 1024), vmem(ROWS, NVIR),
            vmem(NVIR, 1024), vmem(NVIR, 1024), vmem(1 if tight else 2, 4 * half, NVIR), vmem(1024, NVIR),
            pltpu.SemaphoreType.DMA((SEMS,)), pltpu.SemaphoreType.DMA((SEMS,)), pltpu.SemaphoreType.DMA((4,)),
        ],
        compiler_params=pltpu.CompilerParams(
            collective_id=2 if tight else 3, has_side_effects=True, vmem_limit_bytes=56 << 20
        ),
        name="narrow%d" % packed_rows,
    )(amplitudes, integrals, irreps)


def per_device(amplitudes, integrals, irreps):
    ahead = jnp.pad(irreps, (0, 64), constant_values=-1)
    over = (irreps[:-128] == irreps[128:]).astype(jnp.int32) + (irreps[:-128] == ahead[192:]).astype(jnp.int32)
    kernels = [functools.partial(narrow_ladder, 192), functools.partial(narrow_ladder, 288), functools.partial(ladder, 320)]
    return lax.switch(jnp.max(over), kernels, amplitudes, integrals, irreps)


def solution(mesh):
    placed = (P("pair", "virt"), P("pair", "virt"), P())
    return jax.shard_map(
        per_device, mesh=mesh, in_specs=placed, out_specs=P("pair", "virt"), check_vma=False
    )
```
